32 devices in a mesh: gx: 4 (over z), gy: 8 (over y, x, core).
Axes of the slice: x: 2, y: 2, z: 4, core: 2. Of those that a mesh axis runs over, the one named last changes fastest.
Arguments:
- velocity: float32 [2, 2048, 4096], P(None, 'gx', 'gy'), may hold values from -6 to 6
- observed: float32 [2, 2048, 4096], P(None, 'gx', 'gy'), may hold values from -6 to 6
- thickness: float32 [2048, 4096], P('gx', 'gy'), may hold values from 0.5 to 2
- rate_factor: float32 [2048, 4096], P('gx', 'gy'), may hold values from 0.5 to 2
- friction: float32 [2048, 4096], P('gx', 'gy'), may hold values from 0.1 to 10
- cell_mask: int32 [2048, 4096], P('gx', 'gy'), may hold values from 0 to 2
- front_codes: int32 [2048, 4096], P('gx', 'gy'), may hold values from 0 to 15
- modes_x: bfloat16 [2048, 512], P('gx'), may hold values from -0.125 to 0.125
- modes_y: bfloat16 [4096, 512], P('gy'), may hold values from -0.09375 to 0.09375
Outputs:
- adjoint: float32 [2, 2048, 4096], P(None, 'gx', 'gy')
- coefficients: float32 [512, 512], P('gx', 'gy')
The draws below stay inside these ranges and needn't reach their ends.
Inputs may be any that keep to these rules, and one draw needn't show every extreme that they name: `cell_mask`: 0 is ocean, 1 floating ice, 2 grounded ice. `front_codes`: bit 0, 1, 2, 3 marks a calving front on the cell's lower first-dimension, upper first-dimension, lower second-dimension, upper second-dimension face.
All inputs are finite; a program needn't handle non-finite values.
Results may differ from the reference program's by a relative error of at most 0.0029.
Values sent between devices are 32-bit elements; how exact they have to be, the bound alone decides.
A program may use at most 128 MiB of HBM per device.

```python
import math
import jax
import jax.numpy as jnp
from jax import lax

KM = 512
SWEEPS = 3
NX = 2048
NY = 4096


def place_ends(values, stream_key, smallest, high):
    spot = [jax.random.randint(jax.random.fold_in(stream_key, axis), (), 0, length) for axis, length in enumerate(values.shape)]
    longest = values.shape.index(max(values.shape))
    next_to = spot[:longest] + [(spot[longest] + 1) % values.shape[longest]] + spot[longest + 1:]
    return values.at[tuple(spot)].set(smallest).at[tuple(next_to)].set(high)


def level_of(stream_key, extent, shards, low, top_value):
    def one(axis_at, parts):
        heights = jax.random.uniform(jax.random.fold_in(jax.random.fold_in(stream_key, 6), axis_at), (parts,), jnp.float32, low / len(shards), top_value / len(shards))
        return jnp.repeat(jnp.exp(heights), extent[axis_at] // parts).reshape((-1,) + (1,) * (len(extent) - axis_at - 1))

    level = one(*shards[0])
    for cut in shards[1:]:
        level = level * one(*cut)
    return level


def centred(rng, extent, spread, limit, shards=(), kind=jnp.bfloat16):
    result = spread * jax.random.normal(rng, extent, jnp.float32)
    if shards:
        result = result * level_of(rng, extent, shards, -0.22, 0.18)
    return jnp.clip(result, -limit, limit).astype(kind)


def setup_inputs(seed: int = 0) -> dict:
    keys = jax.random.split(jax.random.key(seed), 10)
    return {
        "velocity": centred(keys[0], (2, NX, NY), 1.0, 6.0, ((1, 4), (2, 8)), jnp.float32),
        "observed": centred(keys[1], (2, NX, NY), 1.0, 6.0, ((1, 4), (2, 8)), jnp.float32),
        "thickness": jnp.clip(jnp.exp(math.log(2.0) - 1.3862944 * jax.random.uniform(keys[2], (NX, NY), jnp.float32) ** level_of(keys[2], (NX, NY), ((0, 4), (1, 8)), -0.2, 0.2)), 0.5, 2.0),
        "rate_factor": jnp.clip(jnp.exp(math.log(2.0) - 1.3862944 * jax.random.uniform(keys[3], (NX, NY), jnp.float32) ** level_of(keys[3], (NX, NY), ((0, 4), (1, 8)), -0.2, 0.2)), 0.5, 2.0),
        "friction": jnp.clip(jnp.exp(math.log(10.0) - 4.6051702 * jax.random.uniform(keys[4], (NX, NY), jnp.float32) ** level_of(keys[4], (NX, NY), ((0, 4), (1, 8)), -0.2, 0.2)), 0.1, 10.0),
        "cell_mask": place_ends(jax.random.randint(keys[5], (NX, NY), 0, 3), jax.random.fold_in(keys[5], 1), 0, 2).astype(jnp.int32),
        "front_codes": place_ends(jax.random.randint(keys[6], (NX, NY), 0, 16), jax.random.fold_in(keys[6], 1), 0, 15).astype(jnp.int32),
        "modes_x": centred(keys[7], (NX, KM), NX ** -0.5, 0.125, ((0, 4),)),
        "modes_y": centred(keys[8], (NY, KM), NY ** -0.5, 0.09375, ((0, 8),)),
    }


def viscosity(padded, stiffness):
    along_x = (padded[:, 2:, 1:-1] - padded[:, :-2, 1:-1]) * 0.5
    along_y = (padded[:, 1:-1, 2:] - padded[:, 1:-1, :-2]) * 0.5
    shear = along_y[0] + along_x[1]
    strain = along_x[0] * along_x[0] + along_y[1] * along_y[1] + along_x[0] * along_y[1] + 0.25 * shear * shear
    return stiffness * 0.5 * (strain + 0.01) ** (-1.0 / 3.0)

def face_terms(eta_pad):
    center = eta_pad[1:-1, 1:-1]
    lower_x = jnp.sqrt(center * eta_pad[:-2, 1:-1])
    upper_x = jnp.sqrt(center * eta_pad[2:, 1:-1])
    lower_y = jnp.sqrt(center * eta_pad[1:-1, :-2])
    upper_y = jnp.sqrt(center * eta_pad[1:-1, 2:])
    return (lower_x, upper_x, lower_y, upper_y)

def front_count(front_codes):
    total = jnp.zeros(front_codes.shape, jnp.float32)
    for bit_index in range(4):
        total = total + (jnp.right_shift(front_codes, bit_index) & 1).astype(jnp.float32)
    return total

def relax(adjoint_pad, faces, rhs, diagonal_sum):
    lower_x, upper_x, lower_y, upper_y = faces
    x_weights = jnp.array([4.0, 1.0], jnp.float32).reshape(2, 1, 1)
    y_weights = jnp.array([1.0, 4.0], jnp.float32).reshape(2, 1, 1)
    near_x = lower_x * adjoint_pad[:, :-2, 1:-1] + upper_x * adjoint_pad[:, 2:, 1:-1]
    near_y = lower_y * adjoint_pad[:, 1:-1, :-2] + upper_y * adjoint_pad[:, 1:-1, 2:]
    return (rhs + x_weights * near_x + y_weights * near_y) / diagonal_sum

def reference(velocity, observed, thickness, rate_factor, friction, cell_mask, front_codes, modes_x, modes_y):
    ice = (cell_mask >= 1).astype(jnp.float32)
    grounded = (cell_mask == 2).astype(jnp.float32)
    stiffness = thickness * ice * rate_factor
    vel_pad = jnp.pad(velocity, ((0, 0), (1, 1), (1, 1)))
    eta = viscosity(vel_pad, stiffness)
    eta_pad = jnp.pad(eta, ((1, 1), (1, 1)))
    faces = face_terms(eta_pad)
    lower_x, upper_x, lower_y, upper_y = faces
    x_weights = jnp.array([4.0, 1.0], jnp.float32).reshape(2, 1, 1)
    y_weights = jnp.array([1.0, 4.0], jnp.float32).reshape(2, 1, 1)
    extra = 2.0 * eta * front_count(front_codes) + friction * grounded + 1.0
    diagonal_sum = x_weights * (lower_x + upper_x) + y_weights * (lower_y + upper_y) + extra
    rhs = ice * (velocity - observed)
    adjoint = rhs / diagonal_sum
    for sweep in range(SWEEPS - 1):
        adjoint_pad = jnp.pad(adjoint, ((0, 0), (1, 1), (1, 1)))
        adjoint = relax(adjoint_pad, faces, rhs, diagonal_sum)
    gradient = (-(friction * grounded) * (velocity[0] * adjoint[0] + velocity[1] * adjoint[1])).astype(jnp.bfloat16)
    partial_rows = lax.dot_general(modes_x, gradient, (((0,), (0,)), ((), ())), preferred_element_type=jnp.float32)
    coefficients = jnp.dot(partial_rows, modes_y.astype(jnp.float32), precision=lax.Precision.HIGHEST)
    return (adjoint, coefficients)
```

```python
import functools

import jax
import jax.numpy as jnp
from jax import lax
from jax.experimental import pallas as pl
from jax.experimental.pallas import tpu as pltpu
from jax.sharding import PartitionSpec as P

SWEEPS = 3
LT = 128
LANES = 8
GROUPS = LT // LANES
TOP = 16
ROWS = 16
BLOCK = 128
FIELDS = 7
VMEM_LIMIT = 56 * 1024 * 1024
MESH = pl.DeviceIdType.MESH
F32 = jnp.float32
BF16 = jnp.bfloat16
U, V, ROOT, DRAG, FRONTS, RHS = 0, 1, 2, 3, 4, 5


def kernel(
    ngx, ngy,
    vel_h, obs_h, thick_h, rate_h, fric_h, mask_h, codes_h, mx_h, my_h,
    adj, coef_ref,
    d, raw_f, raw_i, mx, my, myt,
    ns_vel, ns_f, ns_i, pk_out, pk_in, corner_in,
    s_pad, q1, q2, p_f, g_f, grad,
    y_send, y_in, y_acc, g_in, z_out, z_in,
    load_sem, modes_sem, ns_send, ns_recv, pk_send, pk_recv, corner_send, corner_recv,
    y_ssem, y_rsem, g_ssem, g_rsem, z_send, z_recv,
):
    nt, h, _ = raw_i.shape[1:]
    w = nt * LT
    ring = nt + 1
    group = h // GROUPS
    ix, iy = lax.axis_index("gx"), lax.axis_index("gy")
    edge_tiles, inner_tiles = (0, nt - 1), tuple(range(1, nt - 1))

    def cols(t):
        return pl.ds(t * LT, LT)

    loads = {}
    for t in edge_tiles + inner_tiles:
        pairs = [
            (vel_h.at[:, :, cols(t)], d.at[pl.ds(U, 2), t, pl.ds(TOP, h)]),
            (obs_h.at[:, :, cols(t)], raw_f.at[pl.ds(3, 2), t]),
            (thick_h.at[:, cols(t)], raw_f.at[0, t]),
            (rate_h.at[:, cols(t)], raw_f.at[1, t]),
            (fric_h.at[:, cols(t)], raw_f.at[2, t]),
            (mask_h.at[:, cols(t)], raw_i.at[0, t]),
            (codes_h.at[:, cols(t)], raw_i.at[1, t]),
        ]
        loads[t] = [pltpu.make_async_copy(src, dst, load_sem.at[t, n]) for n, (src, dst) in enumerate(pairs)]
        for load in loads[t]:
            load.start()
    modes = [pltpu.make_async_copy(my_h, my, modes_sem.at[0]), pltpu.make_async_copy(mx_h, mx, modes_sem.at[1])]
    for load in modes:
        load.start()

    has_n, has_s, has_w, has_e = ix > 0, ix < ngx - 1, iy > 0, iy < ngy - 1
    diagonals = (
        (jnp.logical_and(has_n, has_w), -1, -1),
        (jnp.logical_and(has_n, has_e), -1, 1),
        (jnp.logical_and(has_s, has_w), 1, -1),
        (jnp.logical_and(has_s, has_e), 1, 1),
    )

    barrier = pltpu.get_barrier_semaphore()
    for off in range(1, ngx):
        pl.semaphore_signal(barrier, inc=1, device_id=(lax.rem(ix + off, ngx), iy), device_id_type=MESH)
    for off in range(1, ngy):
        pl.semaphore_signal(barrier, inc=1, device_id=(ix, lax.rem(iy + off, ngy)), device_id_type=MESH)
    near = 0
    for there, dx, dy in diagonals:
        near = near + there.astype(jnp.int32)

        @pl.when(there)
        def _(dx=dx, dy=dy):
            pl.semaphore_signal(barrier, inc=1, device_id=(ix + dx, iy + dy), device_id_type=MESH)

    pl.semaphore_wait(barrier, ngx - 1 + ngy - 1 + near)

    def row_copies(side):
        there, step = ((has_s, 1), (has_n, -1))[side]
        rows = pl.ds((h - 8, 0)[side], 8)
        pairs = [
            (vel_h.at[:, rows], ns_vel.at[side, pl.ds(0, 2)]),
            (obs_h.at[:, rows], ns_vel.at[side, pl.ds(2, 2)]),
            (thick_h.at[rows], ns_f.at[side, 0]),
            (rate_h.at[rows], ns_f.at[side, 1]),
            (fric_h.at[rows], ns_f.at[side, 2]),
            (mask_h.at[rows], ns_i.at[side, 0]),
            (codes_h.at[rows], ns_i.at[side, 1]),
        ]
        return there, [
            pltpu.make_async_remote_copy(
                src, dst, ns_send.at[side, n], ns_recv.at[side, n], device_id=(ix + step, iy), device_id_type=MESH)
            for n, (src, dst) in enumerate(pairs)
        ]

    def pack_copies():
        west = pltpu.make_async_remote_copy(
            pk_out.at[0], pk_in.at[1], pk_send.at[0], pk_recv.at[1], device_id=(ix, iy - 1), device_id_type=MESH)
        east = pltpu.make_async_remote_copy(
            pk_out.at[1], pk_in.at[0], pk_send.at[1], pk_recv.at[0], device_id=(ix, iy + 1), device_id_type=MESH)
        return [(has_w, west), (has_e, east)]

    def corner_copies():
        out = []
        for n, (there, dx, dy) in enumerate(diagonals):
            rows = pl.ds(0 if dx < 0 else group - 8, 8)
            out.append((there, pltpu.make_async_remote_copy(
                pk_out.at[0 if dy < 0 else 1, :, rows], corner_in.at[3 - n],
                corner_send.at[n], corner_recv.at[3 - n], device_id=(ix + dx, iy + dy), device_id_type=MESH)))
        return out

    for side in range(2):
        there, copies = row_copies(side)

        @pl.when(there)
        def _(copies=copies):
            for copy in copies:
                copy.start()

    for missing, side in ((ix == 0, 0), (ix == ngx - 1, 1)):

        @pl.when(missing)
        def _(side=side):
            ns_vel[side] = jnp.zeros(ns_vel.shape[1:], F32)
            ns_f[side] = jnp.zeros(ns_f.shape[1:], F32)
            ns_i[side] = jnp.zeros(ns_i.shape[1:], jnp.int32)

    for missing, side in ((iy == 0, 0), (iy == ngy - 1, 1)):

        @pl.when(missing)
        def _(side=side):
            pk_in[side] = jnp.zeros(pk_in.shape[1:], F32)

    for n, (there, _, _) in enumerate(diagonals):

        @pl.when(jnp.logical_not(there))
        def _(n=n):
            corner_in[n] = jnp.zeros(corner_in.shape[1:], F32)

    def loop(step, first, last, stride=ROWS, unroll=2):
        def one(i, carry):
            step(pl.multiple_of(first + i * stride, 8))
            return carry

        lax.fori_loop(0, (last - first) // stride, one, 0, unroll=unroll)

    def derive(kind, code, thick, rate, fric, vel, obs):
        half = 0.5 * thick * rate
        ice = kind >= 1
        root = jnp.where(ice, half * lax.rsqrt(half), 0.0)
        drag = jnp.where(kind == 2, fric, 0.0)
        pairs = code - (lax.shift_right_logical(code, 1) & 5)
        bits = (pairs & 3) + lax.shift_right_logical(pairs, 2)
        fronts = (2 * bits).astype(F32)
        return root, drag, fronts, jnp.where(ice, vel[0] - obs[0], 0.0), jnp.where(ice, vel[1] - obs[1], 0.0)

    def prepare(tiles):
        def step(r):
            here, there = pl.ds(r, ROWS), pl.ds(r + TOP, ROWS)
            for t in tiles:
                out = derive(
                    raw_i[0, t, here], raw_i[1, t, here], raw_f[0, t, here], raw_f[1, t, here], raw_f[2, t, here],
                    [d[U, t, there], d[V, t, there]], [raw_f[3, t, here], raw_f[4, t, here]])
                for f, value in enumerate(out):
                    d[ROOT + f, t, there] = value

        loop(step, 0, h)

    lane = lax.broadcasted_iota(jnp.int32, (group, LT), 1)
    lane8 = lax.broadcasted_iota(jnp.int32, (8, LT), 1)

    def pack(f, carry):
        for side, t in enumerate(edge_tiles):
            slot = lax.rem(lane + 4 * side, LT) // LANES
            value = None
            for n in range(GROUPS):
                part = d[f, t, pl.ds(TOP + n * group, group)]
                by = LANES * (n + 1) % LT
                part = pltpu.roll(part, by, 1) if by else part
                value = part if value is None else jnp.where(slot == (n + 1) % GROUPS, part, value)
            pk_out[side, f] = value
        return carry

    def unpack(f, carry):
        value = jnp.where(lane % LANES < 4, pk_in[1, f], pk_in[0, f])
        for n in range(GROUPS):
            by = (LT - LANES * (n + 1)) % LT
            d[f, nt, pl.ds(TOP + n * group, group)] = pltpu.roll(value, by, 1) if by else value
        d[f, nt, pl.ds(TOP - 8, 8)] = jnp.where(lane8 < LT // 2, corner_in[1, f], corner_in[0, f])
        low = jnp.where(lane8 % LANES < 4, corner_in[3, f], corner_in[2, f])
        d[f, nt, pl.ds(TOP + h, 8)] = pltpu.roll(low, LT - LANES, 1)
        return carry

    for t in edge_tiles:
        for load in loads[t]:
            load.wait()
    prepare(edge_tiles)
    lax.fori_loop(0, FIELDS, pack, 0)
    for there, copy in pack_copies() + corner_copies():

        @pl.when(there)
        def _(copy=copy):
            copy.start()

    for t in inner_tiles:
        for load in loads[t]:
            load.wait()
    prepare(inner_tiles)
    for load in modes:
        load.wait()
    myt[...] = my[...].T.reshape(myt.shape)

    for side, there in ((0, has_n), (1, has_s)):
        copies = row_copies(side)[1]

        @pl.when(there)
        def _(copies=copies):
            for copy in copies:
                copy.wait_recv()

        rows = pl.ds((TOP - 8, TOP + h)[side], 8)
        for t in range(nt):
            vel = [ns_vel[side, n, :, cols(t)] for n in range(2)]
            out = derive(
                ns_i[side, 0, :, cols(t)], ns_i[side, 1, :, cols(t)],
                ns_f[side, 0, :, cols(t)], ns_f[side, 1, :, cols(t)], ns_f[side, 2, :, cols(t)],
                vel, [ns_vel[side, 2 + n, :, cols(t)] for n in range(2)])
            for f, value in enumerate((*vel, *out)):
                d[f, t, rows] = value

    (_, west), (_, east) = pack_copies()
    for there, copy in ((has_w, east), (has_e, west)):

        @pl.when(there)
        def _(copy=copy):
            copy.wait_recv()

    for (there, _, _), (_, copy) in zip(diagonals, reversed(corner_copies())):

        @pl.when(there)
        def _(copy=copy):
            copy.wait_recv()

    lax.fori_loop(0, FIELDS, unpack, 0)

    lanes = lax.broadcasted_iota(jnp.int32, (ROWS, LT), 1)
    at_first, at_last = lanes == 0, lanes == LT - 1

    def neighbours(ref, c, r, t, kept):
        def turned(tile, by):
            tile = tile % ring
            if (c, tile, by) not in kept:
                kept[c, tile, by] = pltpu.roll(ref[c, tile, pl.ds(r, ROWS)], by, 1)
            return kept[c, tile, by]

        up = ref[c, t, pl.ds(r - 1, ROWS)]
        down = ref[c, t, pl.ds(r + 1, ROWS)]
        left = jnp.where(at_first, turned(t - 1, 1), turned(t, 1))
        right = jnp.where(at_last, turned(t + 1, LT - 1), turned(t, LT - 1))
        return up, down, left, right

    def weighted(ref, c, r, t, kept):
        up, down, left, right = neighbours(ref, c, r, t, kept)
        ns, ew = up + down, left + right
        return 4.0 * ns + ew if c == 0 else ns + 4.0 * ew

    def viscosity(r):
        kept = {}
        for t in range(ring):
            up, down, left, right = neighbours(d, U, r, t, kept)
            ux, uy = down - up, right - left
            up, down, left, right = neighbours(d, V, r, t, kept)
            vx, vy = down - up, right - left
            shear = uy + vx
            strain = 0.25 * (ux * ux + vy * vy + ux * vy + 0.25 * (shear * shear))
            s_pad[0, t, pl.ds(r, ROWS)] = d[ROOT, t, pl.ds(r, ROWS)] * jnp.exp2(jnp.log2(strain + 0.01) * (-1.0 / 6.0))

    def first(r):
        kept = {}
        here = pl.ds(r, ROWS)
        for t in range(ring):
            up, down, left, right = neighbours(s_pad, 0, r, t, kept)
            ns, ew = up + down, left + right
            s = s_pad[0, t, here]
            e = d[FRONTS, t, here] * (s * s) + d[DRAG, t, here] + 1.0
            for c, total in ((0, 4.0 * ns + ew), (1, ns + 4.0 * ew)):
                inverse = 1.0 / (s * total + e)
                value = d[RHS + c, t, here] * inverse
                p_f[c, t, here] = value
                g_f[c, t, here] = s * inverse
                q1[c, t, here] = s * value

    def second(r):
        kept = {}
        here = pl.ds(r, ROWS)
        for t in range(ring):
            s = s_pad[0, t, here]
            for c in range(2):
                q2[c, t, here] = q1[c, t, here] + s * g_f[c, t, here] * weighted(q1, c, r, t, kept)

    def third(r):
        kept = {}
        here, there = pl.ds(r - TOP, ROWS), pl.ds(r, ROWS)
        for t in range(nt):
            flux = None
            for c in range(2):
                value = p_f[c, t, there] + g_f[c, t, there] * weighted(q2, c, r, t, kept)
                adj[c, here, cols(t)] = value
                term = d[c, t, there] * value
                flux = term if flux is None else flux + term
            grad[here, cols(t)] = (-d[DRAG, t, there] * flux).astype(BF16)

    loop(viscosity, TOP - 8, TOP + h + 8, unroll=3)
    loop(first, TOP - 8, TOP + h + 8, unroll=3)
    loop(second, TOP - 8, TOP + h + 8, unroll=3)

    nblk, _, kb, _ = myt.shape
    steps = h // BLOCK
    ab = mx.shape[1] // ngx
    core = lax.rem(iy, 2)
    cell = iy // 2
    rows_dims = (((1,), (1,)), ((), ()))
    order = (nblk - 1, *range(1, nblk - 1))

    def project(side, k):
        rows = myt[:, side].reshape(nblk * kb, w)
        out = lax.dot_general(rows, grad[k * BLOCK : (k + 1) * BLOCK, :], rows_dims, preferred_element_type=F32)
        return out.reshape(nblk, kb, BLOCK)

    def sibling_copy(k):
        return pltpu.make_async_remote_copy(
            y_send.at[k], y_in.at[k], y_ssem.at[k], y_rsem.at[k],
            device_id=(ix, iy + 1 - 2 * core), device_id_type=MESH)

    def plane_copy(k, off):
        other = lax.rem(cell + off, nblk)
        return pltpu.make_async_remote_copy(
            y_acc.at[k, other], g_in.at[k, off - 1], g_ssem.at[k, off - 1], g_rsem.at[k, off - 1],
            device_id=(ix, 2 * other + core), device_id_type=MESH)

    def forward(k):
        sibling_copy(k).wait_recv()
        y_acc[k] += y_in[k]
        for off in range(nblk - 1, 0, -1):
            plane_copy(k, off).start()

    for k in range(steps):
        loop(third, TOP + k * BLOCK, TOP + (k + 1) * BLOCK, unroll=4)
        y_send[k] = project(1 - core, k)
        sibling_copy(k).start()
        y_acc[k] = project(core, k)
        if k:
            forward(k - 1)
    forward(steps - 1)

    total = None
    for k in range(steps):
        rows = y_acc[k, cell]
        for off in range(1, nblk):
            plane_copy(k, off).wait_recv()
            rows = rows + g_in[k, off - 1]
        high = rows.astype(BF16)
        low = (rows - high.astype(F32)).astype(BF16)
        both = jnp.concatenate([high, low], axis=0)
        out = jnp.dot(both, mx[k * BLOCK : (k + 1) * BLOCK, :], preferred_element_type=F32)
        total = out if total is None else total + out
    total = total[:kb] + total[kb:]

    for n in range(ngx):
        z_out[n] = total[:, n * ab : (n + 1) * ab]

    for n in range(ngx):

        @pl.when(ix != n)
        def _(n=n):
            pltpu.make_async_remote_copy(
                z_out.at[n], z_in.at[ix], z_send.at[n], z_recv.at[ix],
                device_id=(n, iy), device_id_type=MESH).start()

    def z_copy(n):
        return pltpu.make_async_remote_copy(
            z_out.at[n], z_in.at[n], z_send.at[n], z_recv.at[n],
            device_id=(n, iy), device_id_type=MESH)

    for side in range(2):
        there, copies = row_copies(side)

        @pl.when(there)
        def _(copies=copies):
            for copy in copies:
                copy.wait_send()

    for there, copy in pack_copies() + corner_copies():

        @pl.when(there)
        def _(copy=copy):
            copy.wait_send()

    for k in range(steps):
        sibling_copy(k).wait_send()
        for off in range(1, nblk):
            plane_copy(k, off).wait_send()

    coef_ref[...] = z_out[ix]
    for n in range(ngx):

        @pl.when(ix != n)
        def _(n=n):
            z_copy(n).wait_recv()
            coef_ref[...] += z_in[n]

    for n in range(ngx):

        @pl.when(ix != n)
        def _(n=n):
            z_copy(n).wait_send()


def write_results(adj, coef, adj_h, coef_h, adj_sem, coef_sem):
    rows = adj.shape[1] // 2
    copies = [pltpu.make_async_copy(coef, coef_h, coef_sem)]
    for n in range(4):
        part = (n % 2, pl.ds(n // 2 * rows, rows))
        copies.append(pltpu.make_async_copy(adj.at[part], adj_h.at[part], adj_sem.at[n]))
    for copy in copies:
        copy.start()
    for copy in copies:
        copy.wait()


def shards(ngx, ngy, velocity, observed, thickness, rate_factor, friction, cell_mask, front_codes, modes_x, modes_y):
    h, w = thickness.shape
    km = modes_x.shape[1]
    nt, nblk, kb, ab = w // LT, ngy // 2, km // ngy, km // ngx
    steps = h // BLOCK
    group = h // GROUPS
    hbm_spec = pl.BlockSpec(memory_space=pltpu.HBM)
    vmem_spec = pl.BlockSpec(memory_space=pltpu.VMEM)
    pad = (nt + 1, h + 2 * TOP, LT)
    dma = pltpu.SemaphoreType.DMA
    args = (velocity, observed, thickness, rate_factor, friction, cell_mask, front_codes, modes_x, modes_y)
    args = [pltpu.with_memory_space_constraint(x, pltpu.HBM) for x in args]
    adjoint, coefficients = pl.pallas_call(
        functools.partial(kernel, ngx, ngy),
        out_shape=(pltpu.VMEM((2, h, w), F32), pltpu.VMEM((kb, ab), F32)),
        in_specs=[hbm_spec] * 9,
        out_specs=(vmem_spec, vmem_spec),
        scratch_shapes=[
            pltpu.VMEM((FIELDS, *pad), F32),
            pltpu.VMEM((5, nt, h, LT), F32),
            pltpu.VMEM((2, nt, h, LT), jnp.int32),
            pltpu.VMEM((h, km), BF16),
            pltpu.VMEM((w, km), BF16),
            pltpu.VMEM((nblk, 2, kb, w), BF16),
            pltpu.VMEM((2, 4, 8, w), F32),
            pltpu.VMEM((2, 3, 8, w), F32),
            pltpu.VMEM((2, 2, 8, w), jnp.int32),
            pltpu.VMEM((2, FIELDS, group, LT), F32),
            pltpu.VMEM((2, FIELDS, group, LT), F32),
            pltpu.VMEM((4, FIELDS, 8, LT), F32),
            pltpu.VMEM((1, *pad), F32),
            pltpu.VMEM((2, *pad), F32),
            pltpu.VMEM((2, *pad), F32),
            pltpu.VMEM((2, *pad), F32),
            pltpu.VMEM((2, *pad), F32),
            pltpu.VMEM((h, w), BF16),
            pltpu.VMEM((steps, nblk, kb, BLOCK), F32),
            pltpu.VMEM((steps, nblk, kb, BLOCK), F32),
            pltpu.VMEM((steps, nblk, kb, BLOCK), F32),
            pltpu.VMEM((steps, nblk - 1, kb, BLOCK), F32),
            pltpu.VMEM((ngx, kb, ab), F32),
            pltpu.VMEM((ngx, kb, ab), F32),
            dma((nt, 7)),
            dma((2,)),
            dma((2, 7)),
            dma((2, 7)),
            dma((2,)),
            dma((2,)),
            dma((4,)),
            dma((4,)),
            dma((steps,)),
            dma((steps,)),
            dma((steps, nblk - 1)),
            dma((steps, nblk - 1)),
            dma((ngx,)),
            dma((ngx,)),
        ],
        compiler_params=pltpu.CompilerParams(
            collective_id=0, has_side_effects=True, vmem_limit_bytes=VMEM_LIMIT
        ),
    )(*args)
    adjoint = pltpu.with_memory_space_constraint(adjoint, pltpu.VMEM)
    coefficients = pltpu.with_memory_space_constraint(coefficients, pltpu.VMEM)
    adjoint, coefficients = pl.pallas_call(
        write_results,
        out_shape=(
            jax.ShapeDtypeStruct((2, h, w), F32),
            jax.ShapeDtypeStruct((kb, ab), F32),
        ),
        in_specs=[vmem_spec, vmem_spec],
        out_specs=(hbm_spec, hbm_spec),
        scratch_shapes=[dma((4,)), dma],
    )(adjoint, coefficients)
    return adjoint, coefficients.T


def solution(mesh):
    tile = P("gx", "gy")
    pair = P(None, "gx", "gy")
    return jax.shard_map(
        functools.partial(shards, mesh.shape["gx"], mesh.shape["gy"]),
        mesh=mesh,
        in_specs=(pair, pair, tile, tile, tile, tile, tile, P("gx", None), P("gy", None)),
        out_specs=(pair, tile),
        check_vma=False,
    )
```

```python
import functools

import jax
import jax.numpy as jnp
from jax import lax
from jax.experimental import pallas as pl
from jax.experimental.pallas import tpu as pltpu
from jax.sharding import PartitionSpec as P

SWEEPS = 3
LT = 128
LANES = 8
GROUPS = LT // LANES
TOP = 16
ROWS = 16
BLOCK = 128
FIELDS = 7
VMEM_LIMIT = 56 * 1024 * 1024
MESH = pl.DeviceIdType.MESH
F32 = jnp.float32
BF16 = jnp.bfloat16
U, V, ROOT, DRAG, FRONTS, RHS = 0, 1, 2, 3, 4, 5


def kernel(
    ngx, ngy,
    vel_h, obs_h, thick_h, rate_h, fric_h, mask_h, codes_h, mx_h, my_h,
    adj, coef_ref,
    d, raw_f, raw_i, mx, my, myt,
    ns_vel, ns_f, ns_i, pk_out, pk_in, corner_in,
    s_pad, q1, q2, p_f, g_f, grad,
    y_send, y_in, y_acc, g_in, z_out, z_in,
    load_sem, modes_sem, ns_send, ns_recv, pk_send, pk_recv, corner_send, corner_recv,
    y_ssem, y_rsem, g_ssem, g_rsem, z_send, z_recv,
):
    nt, h, _ = raw_i.shape[1:]
    w = nt * LT
    ring = nt + 1
    group = h // GROUPS
    ix, iy = lax.axis_index("gx"), lax.axis_index("gy")
    edge_tiles, inner_tiles = (0, nt - 1), tuple(range(1, nt - 1))

    def cols(t):
        return pl.ds(t * LT, LT)

    loads = {}
    for t in edge_tiles + inner_tiles:
        pairs = [
            (vel_h.at[:, :, cols(t)], d.at[pl.ds(U, 2), t, pl.ds(TOP, h)]),
            (obs_h.at[:, :, cols(t)], raw_f.at[pl.ds(3, 2), t]),
            (thick_h.at[:, cols(t)], raw_f.at[0, t]),
            (rate_h.at[:, cols(t)], raw_f.at[1, t]),
            (fric_h.at[:, cols(t)], raw_f.at[2, t]),
            (mask_h.at[:, cols(t)], raw_i.at[0, t]),
            (codes_h.at[:, cols(t)], raw_i.at[1, t]),
        ]
        loads[t] = [pltpu.make_async_copy(src, dst, load_sem.at[t, n]) for n, (src, dst) in enumerate(pairs)]
    for t in edge_tiles:
        loads[t][0].start()
    for t in edge_tiles:
        for load in loads[t][1:]:
            load.start()
    for t in inner_tiles:
        for load in loads[t]:
            load.start()
    modes = [pltpu.make_async_copy(my_h, my, modes_sem.at[0]), pltpu.make_async_copy(mx_h, mx, modes_sem.at[1])]
    for load in modes:
        load.start()

    has_n, has_s, has_w, has_e = ix > 0, ix < ngx - 1, iy > 0, iy < ngy - 1
    diagonals = (
        (jnp.logical_and(has_n, has_w), -1, -1),
        (jnp.logical_and(has_n, has_e), -1, 1),
        (jnp.logical_and(has_s, has_w), 1, -1),
        (jnp.logical_and(has_s, has_e), 1, 1),
    )

    barrier = pltpu.get_barrier_semaphore()
    for off in range(1, ngx):
        pl.semaphore_signal(barrier, inc=1, device_id=(lax.rem(ix + off, ngx), iy), device_id_type=MESH)
    for off in range(1, ngy):
        pl.semaphore_signal(barrier, inc=1, device_id=(ix, lax.rem(iy + off, ngy)), device_id_type=MESH)
    near = 0
    for there, dx, dy in diagonals:
        near = near + there.astype(jnp.int32)

        @pl.when(there)
        def _(dx=dx, dy=dy):
            pl.semaphore_signal(barrier, inc=1, device_id=(ix + dx, iy + dy), device_id_type=MESH)

    def row_copies(side):
        there, step = ((has_s, 1), (has_n, -1))[side]
        rows = pl.ds((h - 8, 0)[side], 8)
        pairs = [
            (vel_h.at[:, rows], ns_vel.at[side, pl.ds(0, 2)]),
            (obs_h.at[:, rows], ns_vel.at[side, pl.ds(2, 2)]),
            (thick_h.at[rows], ns_f.at[side, 0]),
            (rate_h.at[rows], ns_f.at[side, 1]),
            (fric_h.at[rows], ns_f.at[side, 2]),
            (mask_h.at[rows], ns_i.at[side, 0]),
            (codes_h.at[rows], ns_i.at[side, 1]),
        ]
        return there, [
            pltpu.make_async_remote_copy(
                src, dst, ns_send.at[side, n], ns_recv.at[side, n], device_id=(ix + step, iy), device_id_type=MESH)
            for n, (src, dst) in enumerate(pairs)
        ]

    parts = (pl.ds(0, 2), pl.ds(2, FIELDS - 2))

    def pack_copies(part):
        west = pltpu.make_async_remote_copy(
            pk_out.at[0, parts[part]], pk_in.at[1, parts[part]], pk_send.at[part, 0], pk_recv.at[part, 1],
            device_id=(ix, iy - 1), device_id_type=MESH)
        east = pltpu.make_async_remote_copy(
            pk_out.at[1, parts[part]], pk_in.at[0, parts[part]], pk_send.at[part, 1], pk_recv.at[part, 0],
            device_id=(ix, iy + 1), device_id_type=MESH)
        return [(has_w, west), (has_e, east)]

    def corner_copies(part):
        out = []
        for n, (there, dx, dy) in enumerate(diagonals):
            rows = pl.ds(0 if dx < 0 else group - 8, 8)
            out.append((there, pltpu.make_async_remote_copy(
                pk_out.at[0 if dy < 0 else 1, parts[part], rows], corner_in.at[3 - n, parts[part]],
                corner_send.at[part, n], corner_recv.at[part, 3 - n],
                device_id=(ix + dx, iy + dy), device_id_type=MESH)))
        return out

    for missing, side in ((ix == 0, 0), (ix == ngx - 1, 1)):

        @pl.when(missing)
        def _(side=side):
            ns_vel[side] = jnp.zeros(ns_vel.shape[1:], F32)
            ns_f[side] = jnp.zeros(ns_f.shape[1:], F32)
            ns_i[side] = jnp.zeros(ns_i.shape[1:], jnp.int32)

    for missing, side in ((iy == 0, 0), (iy == ngy - 1, 1)):

        @pl.when(missing)
        def _(side=side):
            pk_in[side] = jnp.zeros(pk_in.shape[1:], F32)

    for n, (there, _, _) in enumerate(diagonals):

        @pl.when(jnp.logical_not(there))
        def _(n=n):
            corner_in[n] = jnp.zeros(corner_in.shape[1:], F32)

    def aligned(r, by):
        return r if isinstance(r, int) else pl.multiple_of(r, by)

    def loop(step, first, last, stride=ROWS, unroll=2):
        def one(i, carry):
            step(pl.multiple_of(first + i * stride, 8))
            return carry

        lax.fori_loop(0, (last - first) // stride, one, 0, unroll=unroll)

    def derive(kind, code, thick, rate, fric, vel, obs):
        half = 0.5 * thick * rate
        ice = kind >= 1
        root = jnp.where(ice, half * lax.rsqrt(half), 0.0)
        drag = jnp.where(kind == 2, fric, 0.0)
        pairs = code - (lax.shift_right_logical(code, 1) & 5)
        bits = (pairs & 3) + lax.shift_right_logical(pairs, 2)
        fronts = (2 * bits).astype(F32)
        return root, drag, fronts, jnp.where(ice, vel[0] - obs[0], 0.0), jnp.where(ice, vel[1] - obs[1], 0.0)

    def prepare(tiles):
        def step(r):
            here, there = pl.ds(r, ROWS), pl.ds(r + TOP, ROWS)
            for t in tiles:
                out = derive(
                    raw_i[0, t, here], raw_i[1, t, here], raw_f[0, t, here], raw_f[1, t, here], raw_f[2, t, here],
                    [d[U, t, there], d[V, t, there]], [raw_f[3, t, here], raw_f[4, t, here]])
                for f, value in enumerate(out):
                    d[ROOT + f, t, there] = value

        loop(step, 0, h, unroll=4)

    lane = lax.broadcasted_iota(jnp.int32, (group, LT), 1)
    lane8 = lax.broadcasted_iota(jnp.int32, (8, LT), 1)

    def pack(f, carry):
        for side, t in enumerate(edge_tiles):
            slot = lax.rem(lane + 4 * side, LT) // LANES
            value = None
            for n in range(GROUPS):
                part = d[f, t, pl.ds(TOP + n * group, group)]
                by = LANES * (n + 1) % LT
                part = pltpu.roll(part, by, 1) if by else part
                value = part if value is None else jnp.where(slot == (n + 1) % GROUPS, part, value)
            pk_out[side, f] = value
        return carry

    def unpack(f, carry):
        value = jnp.where(lane % LANES < 4, pk_in[1, f], pk_in[0, f])
        for n in range(GROUPS):
            by = (LT - LANES * (n + 1)) % LT
            d[f, nt, pl.ds(TOP + n * group, group)] = pltpu.roll(value, by, 1) if by else value
        d[f, nt, pl.ds(TOP - 8, 8)] = jnp.where(lane8 < LT // 2, corner_in[1, f], corner_in[0, f])
        low = jnp.where(lane8 % LANES < 4, corner_in[3, f], corner_in[2, f])
        d[f, nt, pl.ds(TOP + h, 8)] = pltpu.roll(low, LT - LANES, 1)
        return carry

    lanes = lax.broadcasted_iota(jnp.int32, (ROWS, LT), 1)
    at_first, at_last = lanes == 0, lanes == LT - 1

    def neighbours(ref, c, r, t, kept):
        def turned(tile, by):
            tile = tile % ring
            if (c, tile, by) not in kept:
                kept[c, tile, by] = pltpu.roll(ref[c, tile, pl.ds(r, ROWS)], by, 1)
            return kept[c, tile, by]

        up = ref[c, t, pl.ds(r - 1, ROWS)]
        down = ref[c, t, pl.ds(r + 1, ROWS)]
        left = jnp.where(at_first, turned(t - 1, 1), turned(t, 1))
        right = jnp.where(at_last, turned(t + 1, LT - 1), turned(t, LT - 1))
        return up, down, left, right

    def weighted(ref, c, r, t, kept):
        up, down, left, right = neighbours(ref, c, r, t, kept)
        ns, ew = up + down, left + right
        return 4.0 * ns + ew if c == 0 else ns + 4.0 * ew

    def viscosity(r):
        kept = {}
        for t in range(ring):
            up, down, left, right = neighbours(d, U, r, t, kept)
            ux, uy = down - up, right - left
            up, down, left, right = neighbours(d, V, r, t, kept)
            vx, vy = down - up, right - left
            shear = uy + vx
            strain = 0.25 * (ux * ux + vy * vy + ux * vy + 0.25 * (shear * shear))
            factor = jnp.exp2(jnp.log2(strain + 0.01) * (-1.0 / 6.0))
            s_pad[0, t, pl.ds(r, ROWS)] = d[ROOT, t, pl.ds(r, ROWS)] * factor if t < nt else factor

    def first(r):
        kept = {}
        here = pl.ds(r, ROWS)
        for t in range(ring):
            up, down, left, right = neighbours(s_pad, 0, r, t, kept)
            ns, ew = up + down, left + right
            s = s_pad[0, t, here]
            e = d[FRONTS, t, here] * (s * s) + d[DRAG, t, here] + 1.0
            for c, total in ((0, 4.0 * ns + ew), (1, ns + 4.0 * ew)):
                inverse = 1.0 / (s * total + e)
                value = d[RHS + c, t, here] * inverse
                p_f[c, t, here] = value
                g_f[c, t, here] = s * inverse
                q1[c, t, here] = s * value

    def second(r):
        kept = {}
        here = pl.ds(r, ROWS)
        for t in range(ring):
            s = s_pad[0, t, here]
            for c in range(2):
                q2[c, t, here] = q1[c, t, here] + s * g_f[c, t, here] * weighted(q1, c, r, t, kept)

    def third(r):
        kept = {}
        here, there = pl.ds(aligned(r - TOP, ROWS), ROWS), pl.ds(r, ROWS)
        for t in range(nt):
            flux = None
            for c in range(2):
                value = p_f[c, t, there] + g_f[c, t, there] * weighted(q2, c, r, t, kept)
                adj[c, here, cols(t)] = value
                term = d[c, t, there] * value
                flux = term if flux is None else flux + term
            grad[here, cols(t)] = (-d[DRAG, t, there] * flux).astype(BF16)

    nblk, _, kb, _ = myt.shape
    steps = h // BLOCK
    ab = mx.shape[1] // ngx
    core = lax.rem(iy, 2)
    cell = iy // 2
    rows_dims = (((1,), (1,)), ((), ()))
    order = (nblk - 1, *range(1, nblk - 1))

    def project(side, k):
        rows = myt[:, side].reshape(nblk * kb, w)
        here = pl.ds(pl.multiple_of(k * BLOCK, BLOCK), BLOCK)
        out = lax.dot_general(rows, grad[here, :], rows_dims, preferred_element_type=F32)
        return out.reshape(nblk, kb, BLOCK)

    def sibling_copy(k):
        return pltpu.make_async_remote_copy(
            y_send.at[k], y_in.at[k], y_ssem.at[k], y_rsem.at[k],
            device_id=(ix, iy + 1 - 2 * core), device_id_type=MESH)

    def plane_copy(k, off):
        other = lax.rem(cell + off, nblk)
        return pltpu.make_async_remote_copy(
            y_acc.at[k, other], g_in.at[k, off - 1], g_ssem.at[k, off - 1], g_rsem.at[k, off - 1],
            device_id=(ix, 2 * other + core), device_id_type=MESH)

    def forward(k):
        sibling_copy(k).wait_recv()
        y_acc[k] += y_in[k]
        for off in range(nblk - 1, 0, -1):
            plane_copy(k, off).start()

    def start_sides(part):
        for there, copy in pack_copies(part) + corner_copies(part):

            @pl.when(there)
            def _(copy=copy):
                copy.start()

    def take_sides(part):
        (_, west), (_, east) = pack_copies(part)
        waits = [(has_w, east), (has_e, west)]
        waits += [(there, copy) for (there, _, _), (_, copy) in zip(diagonals, reversed(corner_copies(part)))]
        for there, copy in waits:

            @pl.when(there)
            def _(copy=copy):
                copy.wait_recv()

    for t in edge_tiles:
        loads[t][0].wait()
    lax.fori_loop(0, 2, pack, 0)
    pl.semaphore_wait(barrier, ngx - 1 + ngy - 1 + near)
    start_sides(0)
    for side in range(2):
        there, copies = row_copies(side)

        @pl.when(there)
        def _(copies=copies):
            for copy in copies:
                copy.start()

    for t in edge_tiles:
        for load in loads[t][1:]:
            load.wait()
    prepare(edge_tiles)
    lax.fori_loop(2, FIELDS, pack, 0)
    start_sides(1)

    for t in inner_tiles:
        for load in loads[t]:
            load.wait()
    prepare(inner_tiles)
    for load in modes:
        load.wait()
    myt[...] = my[...].T.reshape(myt.shape)

    take_sides(0)
    lax.fori_loop(0, 2, unpack, 0)
    loop(viscosity, TOP + 8, TOP + h - 8, unroll=8)

    for side, there in ((0, has_n), (1, has_s)):
        copies = row_copies(side)[1]

        @pl.when(there)
        def _(copies=copies):
            for copy in copies:
                copy.wait_recv()

        rows = pl.ds((TOP - 8, TOP + h)[side], 8)
        for t in range(nt):
            vel = [ns_vel[side, n, :, cols(t)] for n in range(2)]
            out = derive(
                ns_i[side, 0, :, cols(t)], ns_i[side, 1, :, cols(t)],
                ns_f[side, 0, :, cols(t)], ns_f[side, 1, :, cols(t)], ns_f[side, 2, :, cols(t)],
                vel, [ns_vel[side, 2 + n, :, cols(t)] for n in range(2)])
            for f, value in enumerate((*vel, *out)):
                d[f, t, rows] = value

    viscosity(TOP - 8)
    viscosity(TOP + h - 8)

    take_sides(1)
    lax.fori_loop(2, FIELDS, unpack, 0)
    ringed = pl.ds(TOP - 8, h + 16)
    s_pad[0, nt, ringed] = s_pad[0, nt, ringed] * d[ROOT, nt, ringed]

    def wave(n, parts="tsf"):
        if "t" in parts:
            third(aligned(TOP + (n - 4) * ROWS, ROWS))
        if "s" in parts:
            second(aligned(TOP - 8 + (n - 2) * ROWS, 8))
        if "f" in parts:
            first(aligned(TOP - 8 + n * ROWS, 8))

    per = BLOCK // ROWS
    half = per // 2

    def send_half(k):
        y_send[k] = project(1 - core, k)

    def keep_half(k):
        y_acc[k] = project(core, k)

    for n in range(4):
        wave(n, "f" if n < 2 else "sf")

    def opening(i, carry):
        for n in range(half):
            wave(4 + i * half + n)
        return carry

    lax.fori_loop(0, 2, opening, 0)

    def block(k, carry):
        send_half(k - 1)
        for n in range(half):
            wave(4 + k * per + n)
        sibling_copy(k - 1).start()

        @pl.when(k >= 2)
        def _():
            forward(k - 2)

        keep_half(k - 1)
        for n in range(half):
            wave(4 + k * per + half + n)
        return carry

    lax.fori_loop(1, steps - 1, block, 0)
    last = steps - 1
    send_half(last - 1)
    for n in range(half):
        wave(4 + last * per + n)
    sibling_copy(last - 1).start()
    forward(last - 2)
    keep_half(last - 1)
    for n, parts_of in enumerate(("tsf", "ts", "ts", "t")):
        wave(4 + last * per + half + n, parts_of)
    send_half(last)
    sibling_copy(last).start()
    forward(last - 1)
    keep_half(last)
    forward(last)

    total = None
    for k in range(steps):
        rows = y_acc[k, cell]
        for off in range(1, nblk):
            plane_copy(k, off).wait_recv()
            rows = rows + g_in[k, off - 1]
        high = rows.astype(BF16)
        low = (rows - high.astype(F32)).astype(BF16)
        both = jnp.concatenate([high, low], axis=0)
        out = jnp.dot(both, mx[k * BLOCK : (k + 1) * BLOCK, :], preferred_element_type=F32)
        total = out if total is None else total + out
    total = total[:kb] + total[kb:]

    for n in range(ngx):
        z_out[n] = total[:, n * ab : (n + 1) * ab]

    for n in range(ngx):

        @pl.when(ix != n)
        def _(n=n):
            pltpu.make_async_remote_copy(
                z_out.at[n], z_in.at[ix], z_send.at[n], z_recv.at[ix],
                device_id=(n, iy), device_id_type=MESH).start()

    def z_copy(n):
        return pltpu.make_async_remote_copy(
            z_out.at[n], z_in.at[n], z_send.at[n], z_recv.at[n],
            device_id=(n, iy), device_id_type=MESH)

    for side in range(2):
        there, copies = row_copies(side)

        @pl.when(there)
        def _(copies=copies):
            for copy in copies:
                copy.wait_send()

    for there, copy in pack_copies(0) + corner_copies(0) + pack_copies(1) + corner_copies(1):

        @pl.when(there)
        def _(copy=copy):
            copy.wait_send()

    for k in range(steps):
        sibling_copy(k).wait_send()
        for off in range(1, nblk):
            plane_copy(k, off).wait_send()

    coef_ref[...] = z_out[ix]
    for n in range(ngx):

        @pl.when(ix != n)
        def _(n=n):
            z_copy(n).wait_recv()
            coef_ref[...] += z_in[n]

    for n in range(ngx):

        @pl.when(ix != n)
        def _(n=n):
            z_copy(n).wait_send()


def write_results(adj, coef, adj_h, coef_h, adj_sem, coef_sem):
    rows = adj.shape[1] // 2
    copies = [pltpu.make_async_copy(coef, coef_h, coef_sem)]
    for n in range(4):
        part = (n % 2, pl.ds(n // 2 * rows, rows))
        copies.append(pltpu.make_async_copy(adj.at[part], adj_h.at[part], adj_sem.at[n]))
    for copy in copies:
        copy.start()
    for copy in copies:
        copy.wait()


def shards(ngx, ngy, velocity, observed, thickness, rate_factor, friction, cell_mask, front_codes, modes_x, modes_y):
    h, w = thickness.shape
    km = modes_x.shape[1]
    nt, nblk, kb, ab = w // LT, ngy // 2, km // ngy, km // ngx
    steps = h // BLOCK
    group = h // GROUPS
    hbm_spec = pl.BlockSpec(memory_space=pltpu.HBM)
    vmem_spec = pl.BlockSpec(memory_space=pltpu.VMEM)
    pad = (nt + 1, h + 2 * TOP, LT)
    dma = pltpu.SemaphoreType.DMA
    args = (velocity, observed, thickness, rate_factor, friction, cell_mask, front_codes, modes_x, modes_y)
    args = [pltpu.with_memory_space_constraint(x, pltpu.HBM) for x in args]
    adjoint, coefficients = pl.pallas_call(
        functools.partial(kernel, ngx, ngy),
        out_shape=(pltpu.VMEM((2, h, w), F32), pltpu.VMEM((kb, ab), F32)),
        in_specs=[hbm_spec] * 9,
        out_specs=(vmem_spec, vmem_spec),
        scratch_shapes=[
            pltpu.VMEM((FIELDS, *pad), F32),
            pltpu.VMEM((5, nt, h, LT), F32),
            pltpu.VMEM((2, nt, h, LT), jnp.int32),
            pltpu.VMEM((h, km), BF16),
            pltpu.VMEM((w, km), BF16),
            pltpu.VMEM((nblk, 2, kb, w), BF16),
            pltpu.VMEM((2, 4, 8, w), F32),
            pltpu.VMEM((2, 3, 8, w), F32),
            pltpu.VMEM((2, 2, 8, w), jnp.int32),
            pltpu.VMEM((2, FIELDS, group, LT), F32),
            pltpu.VMEM((2, FIELDS, group, LT), F32),
            pltpu.VMEM((4, FIELDS, 8, LT), F32),
            pltpu.VMEM((1, *pad), F32),
            pltpu.VMEM((2, *pad), F32),
            pltpu.VMEM((2, *pad), F32),
            pltpu.VMEM((2, *pad), F32),
            pltpu.VMEM((2, *pad), F32),
            pltpu.VMEM((h, w), BF16),
            pltpu.VMEM((steps, nblk, kb, BLOCK), F32),
            pltpu.VMEM((steps, nblk, kb, BLOCK), F32),
            pltpu.VMEM((steps, nblk, kb, BLOCK), F32),
            pltpu.VMEM((steps, nblk - 1, kb, BLOCK), F32),
            pltpu.VMEM((ngx, kb, ab), F32),
            pltpu.VMEM((ngx, kb, ab), F32),
            dma((nt, 7)),
            dma((2,)),
            dma((2, 7)),
            dma((2, 7)),
            dma((2, 2)),
            dma((2, 2)),
            dma((2, 4)),
            dma((2, 4)),
            dma((steps,)),
            dma((steps,)),
            dma((steps, nblk - 1)),
            dma((steps, nblk - 1)),
            dma((ngx,)),
            dma((ngx,)),
        ],
        compiler_params=pltpu.CompilerParams(
            collective_id=0, has_side_effects=True, vmem_limit_bytes=VMEM_LIMIT
        ),
    )(*args)
    adjoint = pltpu.with_memory_space_constraint(adjoint, pltpu.VMEM)
    coefficients = pltpu.with_memory_space_constraint(coefficients, pltpu.VMEM)
    adjoint, coefficients = pl.pallas_call(
        write_results,
        out_shape=(
            jax.ShapeDtypeStruct((2, h, w), F32),
            jax.ShapeDtypeStruct((kb, ab), F32),
        ),
        in_specs=[vmem_spec, vmem_spec],
        out_specs=(hbm_spec, hbm_spec),
        scratch_shapes=[dma((4,)), dma],
    )(adjoint, coefficients)
    return adjoint, coefficients.T


def solution(mesh):
    tile = P("gx", "gy")
    pair = P(None, "gx", "gy")
    return jax.shard_map(
        functools.partial(shards, mesh.shape["gx"], mesh.shape["gy"]),
        mesh=mesh,
        in_specs=(pair, pair, tile, tile, tile, tile, tile, P("gx", None), P("gy", None)),
        out_specs=(pair, tile),
        check_vma=False,
    )
```

```python
import functools

import jax
import jax.numpy as jnp
from jax import lax
from jax.experimental import pallas as pl
from jax.experimental.pallas import tpu as pltpu
from jax.sharding import PartitionSpec as P

SWEEPS = 3
LT = 128
DEEP = 4
LANES = 2 * DEEP
GROUPS = LT // LANES
TOP = 16
ROWS = 16
BLOCK = 128
EARLY = 2
FIELDS = 7
VMEM_LIMIT = 56 * 1024 * 1024
MESH = pl.DeviceIdType.MESH
F32 = jnp.float32
BF16 = jnp.bfloat16
U, V, ROOT, DRAG, FRONTS, RHS = 0, 1, 2, 3, 4, 5


def kernel(
    ngx, ngy,
    vel_h, obs_h, thick_h, rate_h, fric_h, mask_h, codes_h, mx_h, my_h,
    adj, coef_ref,
    d, raw_f, raw_i, mx, my, myt,
    ns_vel, ns_f, ns_i, pk_out, pk_in, corner_in,
    s_pad, q1, q2, p_f, g_f, grad,
    y_send, y_in, y_acc, g_in, z_out, z_in,
    load_sem, modes_sem, ns_send, ns_recv, pk_send, pk_recv, corner_send, corner_recv,
    y_ssem, y_rsem, g_ssem, g_rsem, z_send, z_recv,
):
    nt, h, _ = raw_i.shape[1:]
    w = nt * LT
    ring = nt + 1
    group = h // GROUPS
    ix, iy = lax.axis_index("gx"), lax.axis_index("gy")
    edge_tiles, inner_tiles = (0, nt - 1), tuple(range(1, nt - 1))

    def cols(t):
        return pl.ds(t * LT, LT)

    loads = {}
    for t in edge_tiles + inner_tiles:
        pairs = [
            (vel_h.at[:, :, cols(t)], d.at[pl.ds(U, 2), t, pl.ds(TOP, h)]),
            (obs_h.at[:, :, cols(t)], raw_f.at[pl.ds(3, 2), t]),
            (thick_h.at[:, cols(t)], raw_f.at[0, t]),
            (rate_h.at[:, cols(t)], raw_f.at[1, t]),
            (fric_h.at[:, cols(t)], raw_f.at[2, t]),
            (mask_h.at[:, cols(t)], raw_i.at[0, t]),
            (codes_h.at[:, cols(t)], raw_i.at[1, t]),
        ]
        loads[t] = [pltpu.make_async_copy(src, dst, load_sem.at[t, n]) for n, (src, dst) in enumerate(pairs)]
    rigid, extra = (2, 3, 5), (1, 4, 6)
    for t in edge_tiles:
        loads[t][0].start()
    for n in range(1, 7):
        for t in edge_tiles:
            loads[t][n].start()
    for n in (0, *rigid, *extra):
        for t in inner_tiles:
            loads[t][n].start()
    modes = [pltpu.make_async_copy(my_h, my, modes_sem.at[0]), pltpu.make_async_copy(mx_h, mx, modes_sem.at[1])]
    for load in modes:
        load.start()

    has_n, has_s, has_w, has_e = ix > 0, ix < ngx - 1, iy > 0, iy < ngy - 1
    diagonals = (
        (jnp.logical_and(has_n, has_w), -1, -1),
        (jnp.logical_and(has_n, has_e), -1, 1),
        (jnp.logical_and(has_s, has_w), 1, -1),
        (jnp.logical_and(has_s, has_e), 1, 1),
    )

    barrier = pltpu.get_barrier_semaphore()
    for off in range(1, ngx):
        pl.semaphore_signal(barrier, inc=1, device_id=(lax.rem(ix + off, ngx), iy), device_id_type=MESH)
    for off in range(1, ngy):
        pl.semaphore_signal(barrier, inc=1, device_id=(ix, lax.rem(iy + off, ngy)), device_id_type=MESH)
    near = 0
    for there, dx, dy in diagonals:
        near = near + there.astype(jnp.int32)

        @pl.when(there)
        def _(dx=dx, dy=dy):
            pl.semaphore_signal(barrier, inc=1, device_id=(ix + dx, iy + dy), device_id_type=MESH)

    def row_copies(side):
        there, step = ((has_s, 1), (has_n, -1))[side]
        rows, to = pl.ds((h - DEEP, 0)[side], DEEP), pl.ds((8 - DEEP, 0)[side], DEEP)
        pairs = [
            (vel_h.at[:, rows], ns_vel.at[side, pl.ds(0, 2), to]),
            (obs_h.at[:, rows], ns_vel.at[side, pl.ds(2, 2), to]),
            (thick_h.at[rows], ns_f.at[side, 0, to]),
            (rate_h.at[rows], ns_f.at[side, 1, to]),
            (fric_h.at[rows], ns_f.at[side, 2, to]),
            (mask_h.at[rows], ns_i.at[side, 0, to]),
            (codes_h.at[rows], ns_i.at[side, 1, to]),
        ]
        return there, [
            pltpu.make_async_remote_copy(
                src, dst, ns_send.at[side, n], ns_recv.at[side, n], device_id=(ix + step, iy), device_id_type=MESH)
            for n, (src, dst) in enumerate(pairs)
        ]

    parts = (pl.ds(0, 2), pl.ds(2, FIELDS - 2))

    def pack_copies(part):
        west = pltpu.make_async_remote_copy(
            pk_out.at[parts[part]], pk_in.at[1, parts[part]], pk_send.at[part, 0], pk_recv.at[part, 1],
            device_id=(ix, iy - 1), device_id_type=MESH)
        east = pltpu.make_async_remote_copy(
            pk_out.at[parts[part]], pk_in.at[0, parts[part]], pk_send.at[part, 1], pk_recv.at[part, 0],
            device_id=(ix, iy + 1), device_id_type=MESH)
        return [(has_w, west), (has_e, east)]

    def corner_copies(part):
        out = []
        for n, (there, dx, dy) in enumerate(diagonals):
            rows = pl.ds(0 if dx < 0 else group - 8, 8)
            out.append((there, pltpu.make_async_remote_copy(
                pk_out.at[parts[part], rows], corner_in.at[3 - n, parts[part]],
                corner_send.at[part, n], corner_recv.at[part, 3 - n],
                device_id=(ix + dx, iy + dy), device_id_type=MESH)))
        return out

    for missing, side in ((ix == 0, 0), (ix == ngx - 1, 1)):

        @pl.when(missing)
        def _(side=side):
            ns_vel[side] = jnp.zeros(ns_vel.shape[1:], F32)
            ns_f[side] = jnp.zeros(ns_f.shape[1:], F32)
            ns_i[side] = jnp.zeros(ns_i.shape[1:], jnp.int32)

    for missing, side in ((iy == 0, 0), (iy == ngy - 1, 1)):

        @pl.when(missing)
        def _(side=side):
            pk_in[side] = jnp.zeros(pk_in.shape[1:], F32)

    for n, (there, _, _) in enumerate(diagonals):

        @pl.when(jnp.logical_not(there))
        def _(n=n):
            corner_in[n] = jnp.zeros(corner_in.shape[1:], F32)

    def aligned(r, by):
        return r if isinstance(r, int) else pl.multiple_of(r, by)

    def loop(step, first, last, stride=ROWS, unroll=2):
        def one(i, carry):
            step(pl.multiple_of(first + i * stride, 8))
            return carry

        lax.fori_loop(0, (last - first) // stride, one, 0, unroll=unroll)

    def root_of(kind, thick, rate):
        half = 0.5 * thick * rate
        return jnp.where(kind >= 1, half * lax.rsqrt(half), 0.0)

    def derive(kind, code, fric, vel, obs):
        ice = kind >= 1
        drag = jnp.where(kind == 2, fric, 0.0)
        pairs = code - (lax.shift_right_logical(code, 1) & 5)
        bits = (pairs & 3) + lax.shift_right_logical(pairs, 2)
        fronts = (2 * bits).astype(F32)
        return drag, fronts, jnp.where(ice, vel[0] - obs[0], 0.0), jnp.where(ice, vel[1] - obs[1], 0.0)

    def raw_root(t, r, rows):
        here = pl.ds(r, rows)
        return root_of(raw_i[0, t, here], raw_f[0, t, here], raw_f[1, t, here])

    def edge_root(side, t):
        return root_of(ns_i[side, 0, :, cols(t)], ns_f[side, 0, :, cols(t)], ns_f[side, 1, :, cols(t)])

    def prepare(tiles, rooted):
        def step(r):
            here, there = pl.ds(r, ROWS), pl.ds(r + TOP, ROWS)
            for t in tiles:
                if rooted:
                    d[ROOT, t, there] = raw_root(t, r, ROWS)
                out = derive(
                    raw_i[0, t, here], raw_i[1, t, here], raw_f[2, t, here],
                    [d[U, t, there], d[V, t, there]], [raw_f[3, t, here], raw_f[4, t, here]])
                for f, value in enumerate(out):
                    d[DRAG + f, t, there] = value

        loop(step, 0, h, unroll=8)

    lane = lax.broadcasted_iota(jnp.int32, (group, LT), 1)
    lane8 = lax.broadcasted_iota(jnp.int32, (8, LT), 1)
    slot = lax.rem(lane + LANES // 2, LT) // LANES

    def pack(f):
        value = None
        for n in range(GROUPS):
            here = pl.ds(TOP + n * group, group)
            part = jnp.where(lane < LT // 2, d[f, 0, here], d[f, nt - 1, here])
            by = LANES * (n + 1) % LT
            part = pltpu.roll(part, by, 1) if by else part
            value = part if value is None else jnp.where(slot == (n + 1) % GROUPS, part, value)
        pk_out[f] = value

    def unpack(f):
        value = jnp.where(lane % LANES < DEEP, pk_in[1, f], pk_in[0, f])
        for n in range(GROUPS):
            by = (LT - LANES * (n + 1)) % LT
            d[f, nt, pl.ds(TOP + n * group, group)] = pltpu.roll(value, by, 1) if by else value
        d[f, nt, pl.ds(TOP - 8, 8)] = jnp.where(lane8 < LT // 2, corner_in[1, f], corner_in[0, f])
        low = jnp.where(lane8 % LANES < DEEP, corner_in[3, f], corner_in[2, f])
        d[f, nt, pl.ds(TOP + h, 8)] = pltpu.roll(low, LT - LANES, 1)


    def neighbours(ref, c, r, t, kept, rows=ROWS):
        lanes = lax.broadcasted_iota(jnp.int32, (rows, LT), 1)

        def turned(tile, by):
            tile = tile % ring
            if (c, tile, by) not in kept:
                kept[c, tile, by] = pltpu.roll(ref[c, tile, pl.ds(r, rows)], by, 1)
            return kept[c, tile, by]

        up = ref[c, t, pl.ds(r - 1, rows)]
        down = ref[c, t, pl.ds(r + 1, rows)]
        left = jnp.where(lanes == 0, turned(t - 1, 1), turned(t, 1))
        right = jnp.where(lanes == LT - 1, turned(t + 1, LT - 1), turned(t, LT - 1))
        return up, down, left, right

    def weighted(ref, c, r, t, kept):
        up, down, left, right = neighbours(ref, c, r, t, kept)
        ns, ew = up + down, left + right
        return 4.0 * ns + ew if c == 0 else ns + 4.0 * ew

    def viscosity(r, rows=ROWS, side=None):
        kept = {}
        here = pl.ds(r, rows)
        for t in range(ring):
            up, down, left, right = neighbours(d, U, r, t, kept, rows)
            ux, uy = down - up, right - left
            up, down, left, right = neighbours(d, V, r, t, kept, rows)
            vx, vy = down - up, right - left
            shear = uy + vx
            strain = 0.25 * (ux * ux + vy * vy + ux * vy + 0.25 * (shear * shear))
            factor = jnp.exp2(jnp.log2(strain + 0.01) * (-1.0 / 6.0))
            if t < nt:
                if side is not None:
                    root = edge_root(side, t)
                elif t in edge_tiles:
                    root = d[ROOT, t, here]
                else:
                    root = raw_root(t, aligned(r - TOP, 8), rows)
                factor = root * factor
            s_pad[0, t, here] = factor

    def first(r):
        kept = {}
        here = pl.ds(r, ROWS)
        for t in range(ring):
            up, down, left, right = neighbours(s_pad, 0, r, t, kept)
            ns, ew = up + down, left + right
            s = s_pad[0, t, here]
            e = d[FRONTS, t, here] * (s * s) + d[DRAG, t, here] + 1.0
            for c, total in ((0, 4.0 * ns + ew), (1, ns + 4.0 * ew)):
                inverse = 1.0 / (s * total + e)
                value = d[RHS + c, t, here] * inverse
                p_f[c, t, here] = value
                g_f[c, t, here] = s * inverse
                q1[c, t, here] = s * value

    def second(r):
        kept = {}
        here = pl.ds(r, ROWS)
        for t in range(ring):
            s = s_pad[0, t, here]
            for c in range(2):
                q2[c, t, here] = q1[c, t, here] + s * g_f[c, t, here] * weighted(q1, c, r, t, kept)

    def third(r):
        kept = {}
        here, there = pl.ds(aligned(r - TOP, ROWS), ROWS), pl.ds(r, ROWS)
        for t in range(nt):
            flux = None
            for c in range(2):
                value = p_f[c, t, there] + g_f[c, t, there] * weighted(q2, c, r, t, kept)
                adj[c, here, cols(t)] = value
                term = d[c, t, there] * value
                flux = term if flux is None else flux + term
            grad[here, cols(t)] = (-d[DRAG, t, there] * flux).astype(BF16)

    nblk, _, kb, _ = myt.shape
    steps = h // BLOCK
    ab = mx.shape[1] // ngx
    core = lax.rem(iy, 2)
    cell = iy // 2
    rows_dims = (((1,), (1,)), ((), ()))
    order = (nblk - 1, *range(1, nblk - 1))

    def project(side, k):
        rows = myt[:, side].reshape(nblk * kb, w)
        here = pl.ds(pl.multiple_of(k * BLOCK, BLOCK), BLOCK)
        out = lax.dot_general(rows, grad[here, :], rows_dims, preferred_element_type=F32)
        return out.reshape(nblk, kb, BLOCK)

    def sibling_copy(k):
        return pltpu.make_async_remote_copy(
            y_send.at[k], y_in.at[k], y_ssem.at[k], y_rsem.at[k],
            device_id=(ix, iy + 1 - 2 * core), device_id_type=MESH)

    def plane_copy(k, off):
        other = lax.rem(cell + off, nblk)
        return pltpu.make_async_remote_copy(
            y_acc.at[k, other], g_in.at[k, off - 1], g_ssem.at[k, off - 1], g_rsem.at[k, off - 1],
            device_id=(ix, 2 * other + core), device_id_type=MESH)

    def forward(k):
        sibling_copy(k).wait_recv()
        y_acc[k] += y_in[k]
        for off in range(nblk - 1, 0, -1):
            plane_copy(k, off).start()

    def start_sides(part):
        for there, copy in pack_copies(part) + corner_copies(part):

            @pl.when(there)
            def _(copy=copy):
                copy.start()

    def take_sides(part):
        (_, west), (_, east) = pack_copies(part)
        waits = [(has_w, east), (has_e, west)]
        waits += [(there, copy) for (there, _, _), (_, copy) in zip(diagonals, reversed(corner_copies(part)))]
        for there, copy in waits:

            @pl.when(there)
            def _(copy=copy):
                copy.wait_recv()

    for t in edge_tiles:
        loads[t][0].wait()
    pack(U)
    pack(V)
    pl.semaphore_wait(barrier, ngx - 1 + ngy - 1 + near)
    start_sides(0)
    for side in range(2):
        there, copies = row_copies(side)

        @pl.when(there)
        def _(copies=copies):
            for copy in copies:
                copy.start()

    for t in edge_tiles:
        for load in loads[t][1:]:
            load.wait()
    prepare(edge_tiles, True)
    for f in range(2, FIELDS):
        pack(f)
    start_sides(1)

    for n in (0, *rigid):
        for t in inner_tiles:
            loads[t][n].wait()
    take_sides(0)
    unpack(U)
    unpack(V)
    tall = (h // ROWS - 2) * ROWS
    loop(viscosity, TOP + 8, TOP + 8 + tall, unroll=10)
    viscosity(TOP + 8 + tall)

    for n in extra:
        for t in inner_tiles:
            loads[t][n].wait()
    prepare(inner_tiles, False)
    for load in modes:
        load.wait()
    myt[...] = my[...].T.reshape(myt.shape)

    for side, there in ((0, has_n), (1, has_s)):
        copies = row_copies(side)[1]

        @pl.when(there)
        def _(copies=copies):
            for copy in copies:
                copy.wait_recv()

        rows = pl.ds((TOP - 8, TOP + h)[side], 8)
        for t in range(nt):
            vel = [ns_vel[side, n, :, cols(t)] for n in range(2)]
            out = derive(
                ns_i[side, 0, :, cols(t)], ns_i[side, 1, :, cols(t)], ns_f[side, 2, :, cols(t)],
                vel, [ns_vel[side, 2 + n, :, cols(t)] for n in range(2)])
            for f, value in zip((U, V, DRAG, FRONTS, RHS, RHS + 1), (*vel, *out)):
                d[f, t, rows] = value

    for side, r in ((0, TOP), (1, TOP + h - 8)):
        viscosity(r, 8)
        viscosity((r - 8, r + 8)[side], 8, side)

    take_sides(1)
    for f in range(2, FIELDS):
        unpack(f)
    ringed = pl.ds(TOP - 8, h + 16)
    s_pad[0, nt, ringed] = s_pad[0, nt, ringed] * d[ROOT, nt, ringed]

    def wave(n, parts="tsf"):
        if "t" in parts:
            third(aligned(TOP + (n - 4) * ROWS, ROWS))
        if "s" in parts:
            second(aligned(TOP - 8 + (n - 2) * ROWS, 8))
        if "f" in parts:
            first(aligned(TOP - 8 + n * ROWS, 8))

    per = BLOCK // ROWS
    half = per // 2

    def send_half(k):
        y_send[k] = project(1 - core, k)

    def keep_half(k):
        y_acc[k] = project(core, k)

    for n in range(4):
        wave(n, "f" if n < 2 else "sf")

    def opening(i, carry):
        for n in range(half):
            wave(4 + i * half + n)
        return carry

    lax.fori_loop(0, 2, opening, 0)

    def block(k, carry):
        send_half(k - 1)
        for n in range(EARLY):
            wave(4 + k * per + n)
        sibling_copy(k - 1).start()

        @pl.when(k >= 2)
        def _():
            forward(k - 2)

        keep_half(k - 1)
        for n in range(EARLY, per):
            wave(4 + k * per + n)
        return carry

    lax.fori_loop(1, steps - 1, block, 0)
    last = steps - 1
    send_half(last - 1)
    for n in range(EARLY):
        wave(4 + last * per + n)
    sibling_copy(last - 1).start()
    forward(last - 2)
    keep_half(last - 1)
    for n in range(EARLY, per):
        wave(4 + last * per + n, {per - 3: "ts", per - 2: "ts", per - 1: "t"}.get(n, "tsf"))
    send_half(last)
    sibling_copy(last).start()
    forward(last - 1)
    keep_half(last)
    forward(last)

    total = None
    for k in range(steps):
        rows = y_acc[k, cell]
        for off in range(1, nblk):
            plane_copy(k, off).wait_recv()
            rows = rows + g_in[k, off - 1]
        high = rows.astype(BF16)
        low = (rows - high.astype(F32)).astype(BF16)
        both = jnp.concatenate([high, low], axis=0)
        out = jnp.dot(both, mx[k * BLOCK : (k + 1) * BLOCK, :], preferred_element_type=F32)
        total = out if total is None else total + out
    total = total[:kb] + total[kb:]

    for n in range(ngx):
        z_out[n] = total[:, n * ab : (n + 1) * ab]

    for off in range(ngx - 1, 0, -1):
        for n in (ix - off, ix + off):

            @pl.when(jnp.logical_and(n >= 0, n < ngx))
            def _(n=n):
                pltpu.make_async_remote_copy(
                    z_out.at[n], z_in.at[ix], z_send.at[n], z_recv.at[ix],
                    device_id=(n, iy), device_id_type=MESH).start()

    def z_copy(n):
        return pltpu.make_async_remote_copy(
            z_out.at[n], z_in.at[n], z_send.at[n], z_recv.at[n],
            device_id=(n, iy), device_id_type=MESH)

    for side in range(2):
        there, copies = row_copies(side)

        @pl.when(there)
        def _(copies=copies):
            for copy in copies:
                copy.wait_send()

    for there, copy in pack_copies(0) + corner_copies(0) + pack_copies(1) + corner_copies(1):

        @pl.when(there)
        def _(copy=copy):
            copy.wait_send()

    for k in range(steps):
        sibling_copy(k).wait_send()
        for off in range(1, nblk):
            plane_copy(k, off).wait_send()

    coef_ref[...] = z_out[ix]
    for n in range(ngx):

        @pl.when(ix != n)
        def _(n=n):
            z_copy(n).wait_recv()
            coef_ref[...] += z_in[n]

    for n in range(ngx):

        @pl.when(ix != n)
        def _(n=n):
            z_copy(n).wait_send()


def write_results(adj, coef, adj_h, coef_h, adj_sem, coef_sem):
    rows = adj.shape[1] // 2
    copies = [pltpu.make_async_copy(coef, coef_h, coef_sem)]
    for n in range(4):
        part = (n % 2, pl.ds(n // 2 * rows, rows))
        copies.append(pltpu.make_async_copy(adj.at[part], adj_h.at[part], adj_sem.at[n]))
    for copy in copies:
        copy.start()
    for copy in copies:
        copy.wait()


def shards(ngx, ngy, velocity, observed, thickness, rate_factor, friction, cell_mask, front_codes, modes_x, modes_y):
    h, w = thickness.shape
    km = modes_x.shape[1]
    nt, nblk, kb, ab = w // LT, ngy // 2, km // ngy, km // ngx
    steps = h // BLOCK
    group = h // GROUPS
    hbm_spec = pl.BlockSpec(memory_space=pltpu.HBM)
    vmem_spec = pl.BlockSpec(memory_space=pltpu.VMEM)
    pad = (nt + 1, h + 2 * TOP, LT)
    dma = pltpu.SemaphoreType.DMA
    args = (velocity, observed, thickness, rate_factor, friction, cell_mask, front_codes, modes_x, modes_y)
    args = [pltpu.with_memory_space_constraint(x, pltpu.HBM) for x in args]
    adjoint, coefficients = pl.pallas_call(
        functools.partial(kernel, ngx, ngy),
        out_shape=(pltpu.VMEM((2, h, w), F32), pltpu.VMEM((kb, ab), F32)),
        in_specs=[hbm_spec] * 9,
        out_specs=(vmem_spec, vmem_spec),
        scratch_shapes=[
            pltpu.VMEM((FIELDS, *pad), F32),
            pltpu.VMEM((5, nt, h, LT), F32),
            pltpu.VMEM((2, nt, h, LT), jnp.int32),
            pltpu.VMEM((h, km), BF16),
            pltpu.VMEM((w, km), BF16),
            pltpu.VMEM((nblk, 2, kb, w), BF16),
            pltpu.VMEM((2, 4, 8, w), F32),
            pltpu.VMEM((2, 3, 8, w), F32),
            pltpu.VMEM((2, 2, 8, w), jnp.int32),
            pltpu.VMEM((FIELDS, group, LT), F32),
            pltpu.VMEM((2, FIELDS, group, LT), F32),
            pltpu.VMEM((4, FIELDS, 8, LT), F32),
            pltpu.VMEM((1, *pad), F32),
            pltpu.VMEM((2, *pad), F32),
            pltpu.VMEM((2, *pad), F32),
            pltpu.VMEM((2, *pad), F32),
            pltpu.VMEM((2, *pad), F32),
            pltpu.VMEM((h, w), BF16),
            pltpu.VMEM((steps, nblk, kb, BLOCK), F32),
            pltpu.VMEM((steps, nblk, kb, BLOCK), F32),
            pltpu.VMEM((steps, nblk, kb, BLOCK), F32),
            pltpu.VMEM((steps, nblk - 1, kb, BLOCK), F32),
            pltpu.VMEM((ngx, kb, ab), F32),
            pltpu.VMEM((ngx, kb, ab), F32),
            dma((nt, 7)),
            dma((2,)),
            dma((2, 7)),
            dma((2, 7)),
            dma((2, 2)),
            dma((2, 2)),
            dma((2, 4)),
            dma((2, 4)),
            dma((steps,)),
            dma((steps,)),
            dma((steps, nblk - 1)),
            dma((steps, nblk - 1)),
            dma((ngx,)),
            dma((ngx,)),
        ],
        compiler_params=pltpu.CompilerParams(
            collective_id=0, has_side_effects=True, vmem_limit_bytes=VMEM_LIMIT
        ),
    )(*args)
    adjoint = pltpu.with_memory_space_constraint(adjoint, pltpu.VMEM)
    coefficients = pltpu.with_memory_space_constraint(coefficients, pltpu.VMEM)
    adjoint, coefficients = pl.pallas_call(
        write_results,
        out_shape=(
            jax.ShapeDtypeStruct((2, h, w), F32),
            jax.ShapeDtypeStruct((kb, ab), F32),
        ),
        in_specs=[vmem_spec, vmem_spec],
        out_specs=(hbm_spec, hbm_spec),
        scratch_shapes=[dma((4,)), dma],
    )(adjoint, coefficients)
    return adjoint, coefficients.T


def solution(mesh):
    tile = P("gx", "gy")
    pair = P(None, "gx", "gy")
    return jax.shard_map(
        functools.partial(shards, mesh.shape["gx"], mesh.shape["gy"]),
        mesh=mesh,
        in_specs=(pair, pair, tile, tile, tile, tile, tile, P("gx", None), P("gy", None)),
        out_specs=(pair, tile),
        check_vma=False,
    )
```

```python
import functools

import jax
import jax.numpy as jnp
from jax import lax
from jax.experimental import pallas as pl
from jax.experimental.pallas import tpu as pltpu
from jax.sharding import PartitionSpec as P

SWEEPS = 3
LT = 128
DEEP = 4
LANES = 2 * DEEP
GROUPS = LT // LANES
TOP = 16
ROWS = 16
BLOCK = 128
EARLY = 2
FIELDS = 7
VMEM_LIMIT = 56 * 1024 * 1024
MESH = pl.DeviceIdType.MESH
F32 = jnp.float32
BF16 = jnp.bfloat16
U, V, ROOT, DRAG, FRONTS, RHS = 0, 1, 2, 3, 4, 5


def kernel(
    ngx, ngy,
    vel_h, obs_h, thick_h, rate_h, fric_h, mask_h, codes_h, mx_h, my_h,
    adj, coef_ref,
    d, raw_f, raw_i, mx, my, myt,
    ns_vel, ns_f, ns_i, pk_out, pk_in, corner_in,
    s_pad, q1, q2, p_f, g_f, grad,
    y_send, y_in, y_acc, g_in, z_out, z_in,
    load_sem, modes_sem, ns_send, ns_recv, pk_send, pk_recv, corner_send, corner_recv,
    y_ssem, y_rsem, g_ssem, g_rsem, z_send, z_recv,
):
    nt, h, _ = raw_i.shape[1:]
    w = nt * LT
    ring = nt + 1
    group = h // GROUPS
    ix, iy = lax.axis_index("gx"), lax.axis_index("gy")
    edge_tiles, inner_tiles = (0, nt - 1), tuple(range(1, nt - 1))

    def cols(t):
        return pl.ds(t * LT, LT)

    has_n, has_s, has_w, has_e = ix > 0, ix < ngx - 1, iy > 0, iy < ngy - 1
    diagonals = (
        (jnp.logical_and(has_n, has_w), -1, -1),
        (jnp.logical_and(has_n, has_e), -1, 1),
        (jnp.logical_and(has_s, has_w), 1, -1),
        (jnp.logical_and(has_s, has_e), 1, 1),
    )

    barrier = pltpu.get_barrier_semaphore()
    for off in range(1, ngx):
        pl.semaphore_signal(barrier, inc=1, device_id=(lax.rem(ix + off, ngx), iy), device_id_type=MESH)
    for off in range(1, ngy):
        pl.semaphore_signal(barrier, inc=1, device_id=(ix, lax.rem(iy + off, ngy)), device_id_type=MESH)
    near = 0
    for there, dx, dy in diagonals:
        near = near + there.astype(jnp.int32)

        @pl.when(there)
        def _(dx=dx, dy=dy):
            pl.semaphore_signal(barrier, inc=1, device_id=(ix + dx, iy + dy), device_id_type=MESH)

    loads = {}
    for t in edge_tiles + inner_tiles:
        pairs = [
            (vel_h.at[:, :, cols(t)], d.at[pl.ds(U, 2), t, pl.ds(TOP, h)]),
            (obs_h.at[:, :, cols(t)], raw_f.at[pl.ds(3, 2), t]),
            (thick_h.at[:, cols(t)], raw_f.at[0, t]),
            (rate_h.at[:, cols(t)], raw_f.at[1, t]),
            (fric_h.at[:, cols(t)], raw_f.at[2, t]),
            (mask_h.at[:, cols(t)], raw_i.at[0, t]),
            (codes_h.at[:, cols(t)], raw_i.at[1, t]),
        ]
        loads[t] = [pltpu.make_async_copy(src, dst, load_sem.at[t, n]) for n, (src, dst) in enumerate(pairs)]
    rigid, extra = (2, 3, 5), (1, 4, 6)
    for t in edge_tiles:
        loads[t][0].start()
    for n in range(1, 7):
        for t in edge_tiles:
            loads[t][n].start()
    for n in (0, *rigid, *extra):
        for t in inner_tiles:
            loads[t][n].start()
    modes = [pltpu.make_async_copy(my_h, my, modes_sem.at[0]), pltpu.make_async_copy(mx_h, mx, modes_sem.at[1])]
    for load in modes:
        load.start()

    def row_copies(side):
        there, step = ((has_s, 1), (has_n, -1))[side]
        rows, to = pl.ds((h - DEEP, 0)[side], DEEP), pl.ds((8 - DEEP, 0)[side], DEEP)
        pairs = [
            (vel_h.at[:, rows], ns_vel.at[side, pl.ds(0, 2), to]),
            (obs_h.at[:, rows], ns_vel.at[side, pl.ds(2, 2), to]),
            (thick_h.at[rows], ns_f.at[side, 0, to]),
            (rate_h.at[rows], ns_f.at[side, 1, to]),
            (fric_h.at[rows], ns_f.at[side, 2, to]),
            (mask_h.at[rows], ns_i.at[side, 0, to]),
            (codes_h.at[rows], ns_i.at[side, 1, to]),
        ]
        return there, [
            pltpu.make_async_remote_copy(
                src, dst, ns_send.at[side, n], ns_recv.at[side, n], device_id=(ix + step, iy), device_id_type=MESH)
            for n, (src, dst) in enumerate(pairs)
        ]

    parts = (pl.ds(0, 2), pl.ds(2, FIELDS - 2))

    def pack_copies(part):
        west = pltpu.make_async_remote_copy(
            pk_out.at[parts[part]], pk_in.at[1, parts[part]], pk_send.at[part, 0], pk_recv.at[part, 1],
            device_id=(ix, iy - 1), device_id_type=MESH)
        east = pltpu.make_async_remote_copy(
            pk_out.at[parts[part]], pk_in.at[0, parts[part]], pk_send.at[part, 1], pk_recv.at[part, 0],
            device_id=(ix, iy + 1), device_id_type=MESH)
        return [(has_w, west), (has_e, east)]

    def corner_copies(part):
        out = []
        for n, (there, dx, dy) in enumerate(diagonals):
            rows = pl.ds(0 if dx < 0 else group - 8, 8)
            out.append((there, pltpu.make_async_remote_copy(
                pk_out.at[parts[part], rows], corner_in.at[3 - n, parts[part]],
                corner_send.at[part, n], corner_recv.at[part, 3 - n],
                device_id=(ix + dx, iy + dy), device_id_type=MESH)))
        return out

    for missing, side in ((ix == 0, 0), (ix == ngx - 1, 1)):

        @pl.when(missing)
        def _(side=side):
            ns_vel[side] = jnp.zeros(ns_vel.shape[1:], F32)
            ns_f[side] = jnp.zeros(ns_f.shape[1:], F32)
            ns_i[side] = jnp.zeros(ns_i.shape[1:], jnp.int32)

    for missing, side in ((iy == 0, 0), (iy == ngy - 1, 1)):

        @pl.when(missing)
        def _(side=side):
            pk_in[side] = jnp.zeros(pk_in.shape[1:], F32)

    for n, (there, _, _) in enumerate(diagonals):

        @pl.when(jnp.logical_not(there))
        def _(n=n):
            corner_in[n] = jnp.zeros(corner_in.shape[1:], F32)

    def aligned(r, by):
        return r if isinstance(r, int) else pl.multiple_of(r, by)

    def loop(step, first, last, stride=ROWS, unroll=2):
        def one(i, carry):
            step(pl.multiple_of(first + i * stride, 8))
            return carry

        lax.fori_loop(0, (last - first) // stride, one, 0, unroll=unroll)

    def root_of(kind, thick, rate):
        half = 0.5 * thick * rate
        return jnp.where(kind >= 1, half * lax.rsqrt(half), 0.0)

    def derive(kind, code, fric, vel, obs):
        ice = kind >= 1
        drag = jnp.where(kind == 2, fric, 0.0)
        pairs = code - (lax.shift_right_logical(code, 1) & 5)
        bits = (pairs & 3) + lax.shift_right_logical(pairs, 2)
        fronts = (2 * bits).astype(F32)
        return drag, fronts, jnp.where(ice, vel[0] - obs[0], 0.0), jnp.where(ice, vel[1] - obs[1], 0.0)

    def raw_root(t, r, rows):
        here = pl.ds(r, rows)
        return root_of(raw_i[0, t, here], raw_f[0, t, here], raw_f[1, t, here])

    def edge_root(side, t):
        return root_of(ns_i[side, 0, :, cols(t)], ns_f[side, 0, :, cols(t)], ns_f[side, 1, :, cols(t)])

    def prepare(tiles, rooted):
        def step(r):
            here, there = pl.ds(r, ROWS), pl.ds(r + TOP, ROWS)
            for t in tiles:
                if rooted:
                    d[ROOT, t, there] = raw_root(t, r, ROWS)
                out = derive(
                    raw_i[0, t, here], raw_i[1, t, here], raw_f[2, t, here],
                    [d[U, t, there], d[V, t, there]], [raw_f[3, t, here], raw_f[4, t, here]])
                for f, value in enumerate(out):
                    d[DRAG + f, t, there] = value

        loop(step, 0, h, unroll=8)

    lane = lax.broadcasted_iota(jnp.int32, (group, LT), 1)
    lane8 = lax.broadcasted_iota(jnp.int32, (8, LT), 1)
    slot = lax.rem(lane + LANES // 2, LT) // LANES

    def pack(f):
        value = None
        for n in range(GROUPS):
            here = pl.ds(TOP + n * group, group)
            part = jnp.where(lane < LT // 2, d[f, 0, here], d[f, nt - 1, here])
            by = LANES * (n + 1) % LT
            part = pltpu.roll(part, by, 1) if by else part
            value = part if value is None else jnp.where(slot == (n + 1) % GROUPS, part, value)
        pk_out[f] = value

    def unpack(f):
        value = jnp.where(lane % LANES < DEEP, pk_in[1, f], pk_in[0, f])
        for n in range(GROUPS):
            by = (LT - LANES * (n + 1)) % LT
            d[f, nt, pl.ds(TOP + n * group, group)] = pltpu.roll(value, by, 1) if by else value
        d[f, nt, pl.ds(TOP - 8, 8)] = jnp.where(lane8 < LT // 2, corner_in[1, f], corner_in[0, f])
        low = jnp.where(lane8 % LANES < DEEP, corner_in[3, f], corner_in[2, f])
        d[f, nt, pl.ds(TOP + h, 8)] = pltpu.roll(low, LT - LANES, 1)


    def neighbours(ref, c, r, t, rows=ROWS):
        lanes = lax.broadcasted_iota(jnp.int32, (rows, LT), 1)

        def near(tile):
            return ref[c, tile % ring, pl.ds(r, rows)]

        up = ref[c, t, pl.ds(r - 1, rows)]
        down = ref[c, t, pl.ds(r + 1, rows)]
        left = pltpu.roll(jnp.where(lanes == LT - 1, near(t - 1), near(t)), 1, 1)
        right = pltpu.roll(jnp.where(lanes == 0, near(t + 1), near(t)), LT - 1, 1)
        return up, down, left, right

    def weighted(ref, c, r, t):
        up, down, left, right = neighbours(ref, c, r, t)
        ns, ew = up + down, left + right
        return 4.0 * ns + ew if c == 0 else ns + 4.0 * ew

    def viscosity(r, rows=ROWS, side=None, tiles=tuple(range(ring))):
        here = pl.ds(r, rows)
        for t in tiles:
            up, down, left, right = neighbours(d, U, r, t, rows)
            ux, uy = down - up, right - left
            up, down, left, right = neighbours(d, V, r, t, rows)
            vx, vy = down - up, right - left
            shear = uy + vx
            strain = 0.25 * (ux * ux + vy * vy + ux * vy + 0.25 * (shear * shear))
            factor = jnp.exp2(jnp.log2(strain + 0.01) * (-1.0 / 6.0))
            if t < nt:
                if side is not None:
                    root = edge_root(side, t)
                elif t in edge_tiles:
                    root = d[ROOT, t, here]
                else:
                    root = raw_root(t, aligned(r - TOP, 8), rows)
                factor = root * factor
            s_pad[0, t, here] = factor

    def first(r):
        here = pl.ds(r, ROWS)
        for t in range(ring):
            up, down, left, right = neighbours(s_pad, 0, r, t)
            ns, ew = up + down, left + right
            s = s_pad[0, t, here]
            e = d[FRONTS, t, here] * (s * s) + d[DRAG, t, here] + 1.0
            for c, total in ((0, 4.0 * ns + ew), (1, ns + 4.0 * ew)):
                inverse = 1.0 / (s * total + e)
                value = d[RHS + c, t, here] * inverse
                p_f[c, t, here] = value
                g_f[c, t, here] = s * inverse
                q1[c, t, here] = s * value

    def second(r):
        here = pl.ds(r, ROWS)
        for t in range(ring):
            s = s_pad[0, t, here]
            for c in range(2):
                q2[c, t, here] = q1[c, t, here] + s * g_f[c, t, here] * weighted(q1, c, r, t)

    def third(r):
        here, there = pl.ds(aligned(r - TOP, ROWS), ROWS), pl.ds(r, ROWS)
        for t in range(nt):
            flux = None
            for c in range(2):
                value = p_f[c, t, there] + g_f[c, t, there] * weighted(q2, c, r, t)
                adj[c, here, cols(t)] = value
                term = d[c, t, there] * value
                flux = term if flux is None else flux + term
            grad[here, cols(t)] = (-d[DRAG, t, there] * flux).astype(BF16)

    nblk, _, kb, _ = myt.shape
    steps = h // BLOCK
    ab = mx.shape[1] // ngx
    core = lax.rem(iy, 2)
    cell = iy // 2
    rows_dims = (((1,), (1,)), ((), ()))

    def project(side, k):
        rows = myt[:, side].reshape(nblk * kb, w)
        here = pl.ds(pl.multiple_of(k * BLOCK, BLOCK), BLOCK)
        out = lax.dot_general(rows, grad[here, :], rows_dims, preferred_element_type=F32)
        return out.reshape(nblk, kb, BLOCK)

    def sibling_copy(k):
        return pltpu.make_async_remote_copy(
            y_send.at[k], y_in.at[k], y_ssem.at[k], y_rsem.at[k],
            device_id=(ix, iy + 1 - 2 * core), device_id_type=MESH)

    def plane_copy(k, off):
        other = cell
        for bit in range(nblk.bit_length() - 1):
            if off >> bit & 1:
                other = other + (1 - 2 * lax.rem(cell // (1 << bit), 2)) * (1 << bit)
        return pltpu.make_async_remote_copy(
            y_acc.at[k, other], g_in.at[k, off - 1], g_ssem.at[k, off - 1], g_rsem.at[k, off - 1],
            device_id=(ix, 2 * other + core), device_id_type=MESH)

    def forward(k):
        sibling_copy(k).wait_recv()
        y_acc[k] += y_in[k]
        for off in range(nblk - 1, 0, -1):
            plane_copy(k, off).start()

    def start_sides(part):
        for there, copy in pack_copies(part) + corner_copies(part):

            @pl.when(there)
            def _(copy=copy):
                copy.start()

    def take_sides(part):
        (_, west), (_, east) = pack_copies(part)
        waits = [(has_w, east), (has_e, west)]
        waits += [(there, copy) for (there, _, _), (_, copy) in zip(diagonals, reversed(corner_copies(part)))]
        for there, copy in waits:

            @pl.when(there)
            def _(copy=copy):
                copy.wait_recv()

    for t in edge_tiles:
        loads[t][0].wait()
    pack(U)
    pack(V)
    pl.semaphore_wait(barrier, ngx - 1 + ngy - 1 + near)
    start_sides(0)
    for side in range(2):
        there, copies = row_copies(side)

        @pl.when(there)
        def _(copies=copies):
            for copy in copies:
                copy.start()

    for t in edge_tiles:
        for load in loads[t][1:]:
            load.wait()
    prepare(edge_tiles, True)
    for f in range(2, FIELDS):
        pack(f)
    start_sides(1)

    for n in (0, *rigid):
        for t in inner_tiles:
            loads[t][n].wait()
    tall = (h // ROWS - 2) * ROWS
    outer = (nt - 1, nt, 0)

    def rough(tiles):
        loop(lambda r: viscosity(r, tiles=tiles), TOP + 8, TOP + 8 + tall, unroll=10)
        viscosity(TOP + 8 + tall, tiles=tiles)

    rough(inner_tiles)
    for n in extra:
        for t in inner_tiles:
            loads[t][n].wait()
    prepare(inner_tiles, False)
    for load in modes:
        load.wait()
    myt[...] = my[...].T.reshape(myt.shape)

    take_sides(0)
    unpack(U)
    unpack(V)
    rough(outer)

    for side, there in ((0, has_n), (1, has_s)):
        copies = row_copies(side)[1]

        @pl.when(there)
        def _(copies=copies):
            for copy in copies:
                copy.wait_recv()

        rows = pl.ds((TOP - 8, TOP + h)[side], 8)
        for t in range(nt):
            vel = [ns_vel[side, n, :, cols(t)] for n in range(2)]
            out = derive(
                ns_i[side, 0, :, cols(t)], ns_i[side, 1, :, cols(t)], ns_f[side, 2, :, cols(t)],
                vel, [ns_vel[side, 2 + n, :, cols(t)] for n in range(2)])
            for f, value in zip((U, V, DRAG, FRONTS, RHS, RHS + 1), (*vel, *out)):
                d[f, t, rows] = value

    for side, r in ((0, TOP), (1, TOP + h - 8)):
        viscosity(r, 8)
        viscosity((r - 8, r + 8)[side], 8, side)

    take_sides(1)
    for f in range(2, FIELDS):
        unpack(f)
    ringed = pl.ds(TOP - 8, h + 16)
    s_pad[0, nt, ringed] = s_pad[0, nt, ringed] * d[ROOT, nt, ringed]

    def wave(n, parts="tsf"):
        if "t" in parts:
            third(aligned(TOP + (n - 4) * ROWS, ROWS))
        if "s" in parts:
            second(aligned(TOP - 8 + (n - 2) * ROWS, 8))
        if "f" in parts:
            first(aligned(TOP - 8 + n * ROWS, 8))

    per = BLOCK // ROWS
    half = per // 2

    def send_half(k):
        y_send[k] = project(1 - core, k)

    def keep_half(k):
        y_acc[k] = project(core, k)

    for n in range(4):
        wave(n, "f" if n < 2 else "sf")

    for n in range(per):
        wave(4 + n)

    def block(k, carry):
        send_half(k - 1)
        for n in range(EARLY):
            wave(4 + k * per + n)
        sibling_copy(k - 1).start()

        @pl.when(k >= 2)
        def _():
            forward(k - 2)

        keep_half(k - 1)
        for n in range(EARLY, per):
            wave(4 + k * per + n)
        return carry

    lax.fori_loop(1, steps - 1, block, 0)
    last = steps - 1
    send_half(last - 1)
    for n in range(EARLY):
        wave(4 + last * per + n)
    sibling_copy(last - 1).start()
    forward(last - 2)
    keep_half(last - 1)
    for n in range(EARLY, per):
        wave(4 + last * per + n, {per - 3: "ts", per - 2: "ts", per - 1: "t"}.get(n, "tsf"))
    send_half(last)
    sibling_copy(last).start()
    forward(last - 1)
    keep_half(last)
    forward(last)

    total = None
    for k in range(steps):
        rows = y_acc[k, cell]
        for off in range(1, nblk):
            plane_copy(k, off).wait_recv()
            rows = rows + g_in[k, off - 1]
        high = rows.astype(BF16)
        low = (rows - high.astype(F32)).astype(BF16)
        both = jnp.concatenate([high, low], axis=0)
        out = jnp.dot(both, mx[k * BLOCK : (k + 1) * BLOCK, :], preferred_element_type=F32)
        total = out if total is None else total + out
    total = total[:kb] + total[kb:]

    for n in range(ngx):
        z_out[n] = total[:, n * ab : (n + 1) * ab]

    for off in range(ngx - 1, 0, -1):
        for n in (ix - off, ix + off):

            @pl.when(jnp.logical_and(n >= 0, n < ngx))
            def _(n=n):
                pltpu.make_async_remote_copy(
                    z_out.at[n], z_in.at[ix], z_send.at[n], z_recv.at[ix],
                    device_id=(n, iy), device_id_type=MESH).start()

    def z_copy(n):
        return pltpu.make_async_remote_copy(
            z_out.at[n], z_in.at[n], z_send.at[n], z_recv.at[n],
            device_id=(n, iy), device_id_type=MESH)

    for side in range(2):
        there, copies = row_copies(side)

        @pl.when(there)
        def _(copies=copies):
            for copy in copies:
                copy.wait_send()

    for there, copy in pack_copies(0) + corner_copies(0) + pack_copies(1) + corner_copies(1):

        @pl.when(there)
        def _(copy=copy):
            copy.wait_send()

    for k in range(steps):
        sibling_copy(k).wait_send()
        for off in range(1, nblk):
            plane_copy(k, off).wait_send()

    coef_ref[...] = z_out[ix]
    for n in range(ngx):

        @pl.when(ix != n)
        def _(n=n):
            z_copy(n).wait_recv()
            coef_ref[...] += z_in[n]

    for n in range(ngx):

        @pl.when(ix != n)
        def _(n=n):
            z_copy(n).wait_send()


def write_results(adj, coef, adj_h, coef_h, adj_sem, coef_sem):
    rows = adj.shape[1] // 2
    copies = [pltpu.make_async_copy(coef, coef_h, coef_sem)]
    for n in range(4):
        part = (n % 2, pl.ds(n // 2 * rows, rows))
        copies.append(pltpu.make_async_copy(adj.at[part], adj_h.at[part], adj_sem.at[n]))
    for copy in copies:
        copy.start()
    for copy in copies:
        copy.wait()


def shards(ngx, ngy, velocity, observed, thickness, rate_factor, friction, cell_mask, front_codes, modes_x, modes_y):
    h, w = thickness.shape
    km = modes_x.shape[1]
    nt, nblk, kb, ab = w // LT, ngy // 2, km // ngy, km // ngx
    steps = h // BLOCK
    group = h // GROUPS
    hbm_spec = pl.BlockSpec(memory_space=pltpu.HBM)
    vmem_spec = pl.BlockSpec(memory_space=pltpu.VMEM)
    pad = (nt + 1, h + 2 * TOP, LT)
    dma = pltpu.SemaphoreType.DMA
    args = (velocity, observed, thickness, rate_factor, friction, cell_mask, front_codes, modes_x, modes_y)
    args = [pltpu.with_memory_space_constraint(x, pltpu.HBM) for x in args]
    adjoint, coefficients = pl.pallas_call(
        functools.partial(kernel, ngx, ngy),
        out_shape=(pltpu.VMEM((2, h, w), F32), pltpu.VMEM((kb, ab), F32)),
        in_specs=[hbm_spec] * 9,
        out_specs=(vmem_spec, vmem_spec),
        scratch_shapes=[
            pltpu.VMEM((FIELDS, *pad), F32),
            pltpu.VMEM((5, nt, h, LT), F32),
            pltpu.VMEM((2, nt, h, LT), jnp.int32),
            pltpu.VMEM((h, km), BF16),
            pltpu.VMEM((w, km), BF16),
            pltpu.VMEM((nblk, 2, kb, w), BF16),
            pltpu.VMEM((2, 4, 8, w), F32),
            pltpu.VMEM((2, 3, 8, w), F32),
            pltpu.VMEM((2, 2, 8, w), jnp.int32),
            pltpu.VMEM((FIELDS, group, LT), F32),
            pltpu.VMEM((2, FIELDS, group, LT), F32),
            pltpu.VMEM((4, FIELDS, 8, LT), F32),
            pltpu.VMEM((1, *pad), F32),
            pltpu.VMEM((2, *pad), F32),
            pltpu.VMEM((2, *pad), F32),
            pltpu.VMEM((2, *pad), F32),
            pltpu.VMEM((2, *pad), F32),
            pltpu.VMEM((h, w), BF16),
            pltpu.VMEM((steps, nblk, kb, BLOCK), F32),
            pltpu.VMEM((steps, nblk, kb, BLOCK), F32),
            pltpu.VMEM((steps, nblk, kb, BLOCK), F32),
            pltpu.VMEM((steps, nblk - 1, kb, BLOCK), F32),
            pltpu.VMEM((ngx, kb, ab), F32),
            pltpu.VMEM((ngx, kb, ab), F32),
            dma((nt, 7)),
            dma((2,)),
            dma((2, 7)),
            dma((2, 7)),
            dma((2, 2)),
            dma((2, 2)),
            dma((2, 4)),
            dma((2, 4)),
            dma((steps,)),
            dma((steps,)),
            dma((steps, nblk - 1)),
            dma((steps, nblk - 1)),
            dma((ngx,)),
            dma((ngx,)),
        ],
        compiler_params=pltpu.CompilerParams(
            collective_id=0, has_side_effects=True, vmem_limit_bytes=VMEM_LIMIT
        ),
    )(*args)
    adjoint = pltpu.with_memory_space_constraint(adjoint, pltpu.VMEM)
    coefficients = pltpu.with_memory_space_constraint(coefficients, pltpu.VMEM)
    adjoint, coefficients = pl.pallas_call(
        write_results,
        out_shape=(
            jax.ShapeDtypeStruct((2, h, w), F32),
            jax.ShapeDtypeStruct((kb, ab), F32),
        ),
        in_specs=[vmem_spec, vmem_spec],
        out_specs=(hbm_spec, hbm_spec),
        scratch_shapes=[dma((4,)), dma],
    )(adjoint, coefficients)
    return adjoint, coefficients.T


def solution(mesh):
    tile = P("gx", "gy")
    pair = P(None, "gx", "gy")
    return jax.shard_map(
        functools.partial(shards, mesh.shape["gx"], mesh.shape["gy"]),
        mesh=mesh,
        in_specs=(pair, pair, tile, tile, tile, tile, tile, P("gx", None), P("gy", None)),
        out_specs=(pair, tile),
        check_vma=False,
    )
```

```python
import functools

import jax
import jax.numpy as jnp
from jax import lax
from jax.experimental import pallas as pl
from jax.experimental.pallas import tpu as pltpu
from jax.sharding import PartitionSpec as P

SWEEPS = 3
LT = 128
DEEP = 4
LANES = 2 * DEEP
GROUPS = LT // LANES
TOP = 16
ROWS = 16
BLOCK = 128
EARLY = 2
FIELDS = 7
VMEM_LIMIT = 56 * 1024 * 1024
MESH = pl.DeviceIdType.MESH
F32 = jnp.float32
BF16 = jnp.bfloat16
U, V, ROOT, DRAG, FRONTS, RHS = 0, 1, 2, 3, 4, 5


def kernel(
    ngx, ngy,
    vel_h, obs_h, thick_h, rate_h, fric_h, mask_h, codes_h, mx_h, my_h,
    adj, coef_ref,
    d, raw_f, raw_i, mx, my, myt,
    ns_vel, ns_f, ns_i, pk_out, pk_in, corner_in,
    s_pad, q1, q2, p_f, g_f, grad,
    y_send, y_in, y_acc, g_in, z_out, z_in,
    load_sem, modes_sem, ns_send, ns_recv, pk_send, pk_recv, corner_send, corner_recv,
    y_ssem, y_rsem, g_ssem, g_rsem, z_send, z_recv,
):
    nt, h, _ = raw_i.shape[1:]
    w = nt * LT
    ring = nt + 1
    group = h // GROUPS
    ix, iy = lax.axis_index("gx"), lax.axis_index("gy")
    edge_tiles, inner_tiles = (0, nt - 1), tuple(range(1, nt - 1))

    def cols(t):
        return pl.ds(t * LT, LT)

    has_n, has_s, has_w, has_e = ix > 0, ix < ngx - 1, iy > 0, iy < ngy - 1
    diagonals = (
        (jnp.logical_and(has_n, has_w), -1, -1),
        (jnp.logical_and(has_n, has_e), -1, 1),
        (jnp.logical_and(has_s, has_w), 1, -1),
        (jnp.logical_and(has_s, has_e), 1, 1),
    )

    barrier = pltpu.get_barrier_semaphore()
    for off in range(1, ngx):
        pl.semaphore_signal(barrier, inc=1, device_id=(lax.rem(ix + off, ngx), iy), device_id_type=MESH)
    for off in range(1, ngy):
        pl.semaphore_signal(barrier, inc=1, device_id=(ix, lax.rem(iy + off, ngy)), device_id_type=MESH)
    near = 0
    for there, dx, dy in diagonals:
        near = near + there.astype(jnp.int32)

        @pl.when(there)
        def _(dx=dx, dy=dy):
            pl.semaphore_signal(barrier, inc=1, device_id=(ix + dx, iy + dy), device_id_type=MESH)

    loads = {}
    for t in edge_tiles + inner_tiles:
        pairs = [
            (vel_h.at[:, :, cols(t)], d.at[pl.ds(U, 2), t, pl.ds(TOP, h)]),
            (obs_h.at[:, :, cols(t)], raw_f.at[pl.ds(3, 2), t]),
            (thick_h.at[:, cols(t)], raw_f.at[0, t]),
            (rate_h.at[:, cols(t)], raw_f.at[1, t]),
            (fric_h.at[:, cols(t)], raw_f.at[2, t]),
            (mask_h.at[:, cols(t)], raw_i.at[0, t]),
            (codes_h.at[:, cols(t)], raw_i.at[1, t]),
        ]
        loads[t] = [pltpu.make_async_copy(src, dst, load_sem.at[t, n]) for n, (src, dst) in enumerate(pairs)]
    rigid, extra = (2, 3, 5), (1, 4, 6)
    for t in edge_tiles:
        loads[t][0].start()
    for n in range(1, 7):
        for t in edge_tiles:
            loads[t][n].start()
    for n in (0, *rigid, *extra):
        for t in inner_tiles:
            loads[t][n].start()
    modes = [pltpu.make_async_copy(my_h, my, modes_sem.at[0]), pltpu.make_async_copy(mx_h, mx, modes_sem.at[1])]
    for load in modes:
        load.start()

    def row_copies(side):
        there, step = ((has_s, 1), (has_n, -1))[side]
        rows, to = pl.ds((h - DEEP, 0)[side], DEEP), pl.ds((8 - DEEP, 0)[side], DEEP)
        pairs = [
            (vel_h.at[:, rows], ns_vel.at[side, pl.ds(0, 2), to]),
            (obs_h.at[:, rows], ns_vel.at[side, pl.ds(2, 2), to]),
            (thick_h.at[rows], ns_f.at[side, 0, to]),
            (rate_h.at[rows], ns_f.at[side, 1, to]),
            (fric_h.at[rows], ns_f.at[side, 2, to]),
            (mask_h.at[rows], ns_i.at[side, 0, to]),
            (codes_h.at[rows], ns_i.at[side, 1, to]),
        ]
        return there, [
            pltpu.make_async_remote_copy(
                src, dst, ns_send.at[side, n], ns_recv.at[side, n], device_id=(ix + step, iy), device_id_type=MESH)
            for n, (src, dst) in enumerate(pairs)
        ]

    parts = (pl.ds(0, 2), pl.ds(2, FIELDS - 2))

    def pack_copies(part):
        west = pltpu.make_async_remote_copy(
            pk_out.at[parts[part]], pk_in.at[1, parts[part]], pk_send.at[part, 0], pk_recv.at[part, 1],
            device_id=(ix, iy - 1), device_id_type=MESH)
        east = pltpu.make_async_remote_copy(
            pk_out.at[parts[part]], pk_in.at[0, parts[part]], pk_send.at[part, 1], pk_recv.at[part, 0],
            device_id=(ix, iy + 1), device_id_type=MESH)
        return [(has_w, west), (has_e, east)]

    def corner_copies(part):
        out = []
        for n, (there, dx, dy) in enumerate(diagonals):
            rows = pl.ds(0 if dx < 0 else group - DEEP, DEEP)
            to = pl.ds(0 if dx < 0 else 8 - DEEP, DEEP)
            out.append((there, pltpu.make_async_remote_copy(
                pk_out.at[parts[part], rows], corner_in.at[3 - n, parts[part], to],
                corner_send.at[part, n], corner_recv.at[part, 3 - n],
                device_id=(ix + dx, iy + dy), device_id_type=MESH)))
        return out

    for missing, side in ((ix == 0, 0), (ix == ngx - 1, 1)):

        @pl.when(missing)
        def _(side=side):
            ns_vel[side] = jnp.zeros(ns_vel.shape[1:], F32)
            ns_f[side] = jnp.zeros(ns_f.shape[1:], F32)
            ns_i[side] = jnp.zeros(ns_i.shape[1:], jnp.int32)

    for missing, side in ((iy == 0, 0), (iy == ngy - 1, 1)):

        @pl.when(missing)
        def _(side=side):
            pk_in[side] = jnp.zeros(pk_in.shape[1:], F32)

    for n, (there, _, _) in enumerate(diagonals):

        @pl.when(jnp.logical_not(there))
        def _(n=n):
            corner_in[n] = jnp.zeros(corner_in.shape[1:], F32)

    def aligned(r, by):
        return r if isinstance(r, int) else pl.multiple_of(r, by)

    def loop(step, first, last, stride=ROWS, unroll=2):
        def one(i, carry):
            step(pl.multiple_of(first + i * stride, 8))
            return carry

        lax.fori_loop(0, (last - first) // stride, one, 0, unroll=unroll)

    def root_of(kind, thick, rate):
        half = 0.5 * thick * rate
        return jnp.where(kind >= 1, half * lax.rsqrt(half), 0.0)

    def derive(kind, code, fric, vel, obs):
        ice = kind >= 1
        drag = jnp.where(kind == 2, fric, 0.0)
        pairs = code - (lax.shift_right_logical(code, 1) & 5)
        bits = (pairs & 3) + lax.shift_right_logical(pairs, 2)
        fronts = (2 * bits).astype(F32)
        return drag, fronts, jnp.where(ice, vel[0] - obs[0], 0.0), jnp.where(ice, vel[1] - obs[1], 0.0)

    def raw_root(t, r, rows):
        here = pl.ds(r, rows)
        return root_of(raw_i[0, t, here], raw_f[0, t, here], raw_f[1, t, here])

    def edge_root(side, t):
        return root_of(ns_i[side, 0, :, cols(t)], ns_f[side, 0, :, cols(t)], ns_f[side, 1, :, cols(t)])

    def prepare(tiles, rooted):
        def step(r):
            here, there = pl.ds(r, ROWS), pl.ds(r + TOP, ROWS)
            for t in tiles:
                if rooted:
                    d[ROOT, t, there] = raw_root(t, r, ROWS)
                out = derive(
                    raw_i[0, t, here], raw_i[1, t, here], raw_f[2, t, here],
                    [d[U, t, there], d[V, t, there]], [raw_f[3, t, here], raw_f[4, t, here]])
                for f, value in enumerate(out):
                    d[DRAG + f, t, there] = value

        loop(step, 0, h, unroll=8)

    lane = lax.broadcasted_iota(jnp.int32, (group, LT), 1)
    lane8 = lax.broadcasted_iota(jnp.int32, (8, LT), 1)
    slot = lax.rem(lane + LANES // 2, LT) // LANES

    def pack(f):
        value = None
        for n in range(GROUPS):
            here = pl.ds(TOP + n * group, group)
            part = jnp.where(lane < LT // 2, d[f, 0, here], d[f, nt - 1, here])
            by = LANES * (n + 1) % LT
            part = pltpu.roll(part, by, 1) if by else part
            value = part if value is None else jnp.where(slot == (n + 1) % GROUPS, part, value)
        pk_out[f] = value

    def unpack(f):
        value = jnp.where(lane % LANES < DEEP, pk_in[1, f], pk_in[0, f])
        for n in range(GROUPS):
            by = (LT - LANES * (n + 1)) % LT
            d[f, nt, pl.ds(TOP + n * group, group)] = pltpu.roll(value, by, 1) if by else value
        d[f, nt, pl.ds(TOP - 8, 8)] = jnp.where(lane8 < LT // 2, corner_in[1, f], corner_in[0, f])
        low = jnp.where(lane8 % LANES < DEEP, corner_in[3, f], corner_in[2, f])
        d[f, nt, pl.ds(TOP + h, 8)] = pltpu.roll(low, LT - LANES, 1)


    def neighbours(ref, c, r, t, rows=ROWS):
        lanes = lax.broadcasted_iota(jnp.int32, (rows, LT), 1)

        def near(tile):
            return ref[c, tile % ring, pl.ds(r, rows)]

        up = ref[c, t, pl.ds(r - 1, rows)]
        down = ref[c, t, pl.ds(r + 1, rows)]
        left = pltpu.roll(jnp.where(lanes == LT - 1, near(t - 1), near(t)), 1, 1)
        right = pltpu.roll(jnp.where(lanes == 0, near(t + 1), near(t)), LT - 1, 1)
        return up, down, left, right

    def weighted(ref, c, r, t):
        up, down, left, right = neighbours(ref, c, r, t)
        ns, ew = up + down, left + right
        return 4.0 * ns + ew if c == 0 else ns + 4.0 * ew

    def viscosity(r, rows=ROWS, side=None, tiles=tuple(range(ring))):
        here = pl.ds(r, rows)
        for t in tiles:
            up, down, left, right = neighbours(d, U, r, t, rows)
            ux, uy = down - up, right - left
            up, down, left, right = neighbours(d, V, r, t, rows)
            vx, vy = down - up, right - left
            shear = uy + vx
            strain = 0.25 * (ux * ux + vy * vy + ux * vy + 0.25 * (shear * shear))
            factor = jnp.exp2(jnp.log2(strain + 0.01) * (-1.0 / 6.0))
            if t < nt:
                if side is not None:
                    root = edge_root(side, t)
                elif t in edge_tiles:
                    root = d[ROOT, t, here]
                else:
                    root = raw_root(t, aligned(r - TOP, 8), rows)
                factor = root * factor
            s_pad[0, t, here] = factor

    def first(r):
        here = pl.ds(r, ROWS)
        for t in range(ring):
            up, down, left, right = neighbours(s_pad, 0, r, t)
            ns, ew = up + down, left + right
            s = s_pad[0, t, here]
            e = d[FRONTS, t, here] * (s * s) + d[DRAG, t, here] + 1.0
            for c, total in ((0, 4.0 * ns + ew), (1, ns + 4.0 * ew)):
                inverse = 1.0 / (s * total + e)
                value = d[RHS + c, t, here] * inverse
                p_f[c, t, here] = value
                g_f[c, t, here] = s * inverse
                q1[c, t, here] = s * value

    def second(r):
        here = pl.ds(r, ROWS)
        for t in range(ring):
            s = s_pad[0, t, here]
            for c in range(2):
                q2[c, t, here] = q1[c, t, here] + s * g_f[c, t, here] * weighted(q1, c, r, t)

    def third(r):
        here, there = pl.ds(aligned(r - TOP, ROWS), ROWS), pl.ds(r, ROWS)
        for t in range(nt):
            flux = None
            for c in range(2):
                value = p_f[c, t, there] + g_f[c, t, there] * weighted(q2, c, r, t)
                adj[c, here, cols(t)] = value
                term = d[c, t, there] * value
                flux = term if flux is None else flux + term
            grad[here, cols(t)] = (-d[DRAG, t, there] * flux).astype(BF16)

    nblk, _, kb, _ = myt.shape
    steps = h // BLOCK
    ab = mx.shape[1] // ngx
    core = lax.rem(iy, 2)
    cell = iy // 2
    rows_dims = (((1,), (1,)), ((), ()))

    def project(side, k):
        rows = myt[:, side].reshape(nblk * kb, w)
        here = pl.ds(pl.multiple_of(k * BLOCK, BLOCK), BLOCK)
        out = lax.dot_general(rows, grad[here, :], rows_dims, preferred_element_type=F32)
        return out.reshape(nblk, kb, BLOCK)

    def sibling_copy(k):
        return pltpu.make_async_remote_copy(
            y_send.at[k], y_in.at[k], y_ssem.at[k], y_rsem.at[k],
            device_id=(ix, iy + 1 - 2 * core), device_id_type=MESH)

    def partner(off):
        other = cell
        for bit in range(nblk.bit_length() - 1):
            if off >> bit & 1:
                other = other + (1 - 2 * lax.rem(cell // (1 << bit), 2)) * (1 << bit)
        return other

    def plane_copy(k, off):
        other = partner(off)
        return pltpu.make_async_remote_copy(
            y_acc.at[k, other], g_in.at[k, off - 1], g_ssem.at[k, off - 1], g_rsem.at[k, off - 1],
            device_id=(ix, 2 * other + core), device_id_type=MESH)

    def forward(k):
        sibling_copy(k).wait_recv()
        for off in range(nblk - 1, 0, -1):
            y_acc[k, partner(off)] += y_in[k, partner(off)]
            plane_copy(k, off).start()

    def start_sides(part):
        for there, copy in pack_copies(part) + corner_copies(part):

            @pl.when(there)
            def _(copy=copy):
                copy.start()

    def take_sides(part):
        (_, west), (_, east) = pack_copies(part)
        waits = [(has_w, east), (has_e, west)]
        waits += [(there, copy) for (there, _, _), (_, copy) in zip(diagonals, reversed(corner_copies(part)))]
        for there, copy in waits:

            @pl.when(there)
            def _(copy=copy):
                copy.wait_recv()

    for t in edge_tiles:
        loads[t][0].wait()
    pack(U)
    pack(V)
    pl.semaphore_wait(barrier, ngx - 1 + ngy - 1 + near)
    start_sides(0)
    for side in range(2):
        there, copies = row_copies(side)

        @pl.when(there)
        def _(copies=copies):
            for copy in copies:
                copy.start()

    for t in edge_tiles:
        for load in loads[t][1:]:
            load.wait()
    prepare(edge_tiles, True)
    for f in range(2, FIELDS):
        pack(f)
    start_sides(1)

    for n in (0, *rigid):
        for t in inner_tiles:
            loads[t][n].wait()
    tall = (h // ROWS - 2) * ROWS
    outer = (nt - 1, nt, 0)

    def rough(tiles):
        loop(lambda r: viscosity(r, tiles=tiles), TOP + 8, TOP + 8 + tall, unroll=10)
        viscosity(TOP + 8 + tall, tiles=tiles)

    rough(inner_tiles)
    for n in extra:
        for t in inner_tiles:
            loads[t][n].wait()
    prepare(inner_tiles, False)
    for load in modes:
        load.wait()
    myt[...] = my[...].T.reshape(myt.shape)

    take_sides(0)
    unpack(U)
    unpack(V)
    rough(outer)

    for side, there in ((0, has_n), (1, has_s)):
        copies = row_copies(side)[1]

        @pl.when(there)
        def _(copies=copies):
            for copy in copies:
                copy.wait_recv()

        rows = pl.ds((TOP - 8, TOP + h)[side], 8)
        for t in range(nt):
            vel = [ns_vel[side, n, :, cols(t)] for n in range(2)]
            out = derive(
                ns_i[side, 0, :, cols(t)], ns_i[side, 1, :, cols(t)], ns_f[side, 2, :, cols(t)],
                vel, [ns_vel[side, 2 + n, :, cols(t)] for n in range(2)])
            for f, value in zip((U, V, DRAG, FRONTS, RHS, RHS + 1), (*vel, *out)):
                d[f, t, rows] = value

    for side, r in ((0, TOP), (1, TOP + h - 8)):
        viscosity(r, 8)
        viscosity((r - 8, r + 8)[side], 8, side)

    take_sides(1)
    for f in range(2, FIELDS):
        unpack(f)
    ringed = pl.ds(TOP - 8, h + 16)
    s_pad[0, nt, ringed] = s_pad[0, nt, ringed] * d[ROOT, nt, ringed]

    def wave(n, parts="tsf"):
        if "t" in parts:
            third(aligned(TOP + (n - 4) * ROWS, ROWS))
        if "s" in parts:
            second(aligned(TOP - 8 + (n - 2) * ROWS, 8))
        if "f" in parts:
            first(aligned(TOP - 8 + n * ROWS, 8))

    per = BLOCK // ROWS
    half = per // 2

    def send_half(k):
        y_send[k] = project(1 - core, k)

    def keep_half(k):
        y_acc[k] = project(core, k)

    for n in range(4):
        wave(n, "f" if n < 2 else "sf")

    for n in range(per):
        wave(4 + n)

    for k in range(1, steps - 1):
        send_half(k - 1)
        for n in range(EARLY):
            wave(4 + k * per + n)
        sibling_copy(k - 1).start()
        if k >= 2:
            forward(k - 2)
        keep_half(k - 1)
        for n in range(EARLY, per):
            wave(4 + k * per + n)

    last = steps - 1
    send_half(last - 1)
    for n in range(EARLY):
        wave(4 + last * per + n)
    sibling_copy(last - 1).start()
    forward(last - 2)
    keep_half(last - 1)
    for n in range(EARLY, per):
        wave(4 + last * per + n, {per - 3: "ts", per - 2: "ts", per - 1: "t"}.get(n, "tsf"))
    send_half(last)
    sibling_copy(last).start()
    forward(last - 1)
    keep_half(last)
    forward(last)

    total = None
    for k in range(steps):
        rows = y_acc[k, cell] + y_in[k, cell]
        for off in range(1, nblk):
            plane_copy(k, off).wait_recv()
            rows = rows + g_in[k, off - 1]
        high = rows.astype(BF16)
        low = (rows - high.astype(F32)).astype(BF16)
        both = jnp.concatenate([high, low], axis=0)
        out = jnp.dot(both, mx[k * BLOCK : (k + 1) * BLOCK, :], preferred_element_type=F32)
        total = out if total is None else total + out
    total = total[:kb] + total[kb:]

    for n in range(ngx):
        z_out[n] = total[:, n * ab : (n + 1) * ab]

    for off in range(ngx - 1, 0, -1):
        for n in (ix - off, ix + off):

            @pl.when(jnp.logical_and(n >= 0, n < ngx))
            def _(n=n):
                pltpu.make_async_remote_copy(
                    z_out.at[n], z_in.at[ix], z_send.at[n], z_recv.at[ix],
                    device_id=(n, iy), device_id_type=MESH).start()

    def z_copy(n):
        return pltpu.make_async_remote_copy(
            z_out.at[n], z_in.at[n], z_send.at[n], z_recv.at[n],
            device_id=(n, iy), device_id_type=MESH)

    for side in range(2):
        there, copies = row_copies(side)

        @pl.when(there)
        def _(copies=copies):
            for copy in copies:
                copy.wait_send()

    for there, copy in pack_copies(0) + corner_copies(0) + pack_copies(1) + corner_copies(1):

        @pl.when(there)
        def _(copy=copy):
            copy.wait_send()

    for k in range(steps):
        sibling_copy(k).wait_send()
        for off in range(1, nblk):
            plane_copy(k, off).wait_send()

    coef_ref[...] = z_out[ix]
    for n in range(ngx):

        @pl.when(ix != n)
        def _(n=n):
            z_copy(n).wait_recv()
            coef_ref[...] += z_in[n]

    for n in range(ngx):

        @pl.when(ix != n)
        def _(n=n):
            z_copy(n).wait_send()


def write_results(adj, coef, adj_h, coef_h, adj_sem, coef_sem):
    rows = adj.shape[1] // 2
    copies = [pltpu.make_async_copy(coef, coef_h, coef_sem)]
    for n in range(4):
        part = (n % 2, pl.ds(n // 2 * rows, rows))
        copies.append(pltpu.make_async_copy(adj.at[part], adj_h.at[part], adj_sem.at[n]))
    for copy in copies:
        copy.start()
    for copy in copies:
        copy.wait()


def shards(ngx, ngy, velocity, observed, thickness, rate_factor, friction, cell_mask, front_codes, modes_x, modes_y):
    h, w = thickness.shape
    km = modes_x.shape[1]
    nt, nblk, kb, ab = w // LT, ngy // 2, km // ngy, km // ngx
    steps = h // BLOCK
    group = h // GROUPS
    hbm_spec = pl.BlockSpec(memory_space=pltpu.HBM)
    vmem_spec = pl.BlockSpec(memory_space=pltpu.VMEM)
    pad = (nt + 1, h + 2 * TOP, LT)
    dma = pltpu.SemaphoreType.DMA
    args = (velocity, observed, thickness, rate_factor, friction, cell_mask, front_codes, modes_x, modes_y)
    args = [pltpu.with_memory_space_constraint(x, pltpu.HBM) for x in args]
    adjoint, coefficients = pl.pallas_call(
        functools.partial(kernel, ngx, ngy),
        out_shape=(pltpu.VMEM((2, h, w), F32), pltpu.VMEM((kb, ab), F32)),
        in_specs=[hbm_spec] * 9,
        out_specs=(vmem_spec, vmem_spec),
        scratch_shapes=[
            pltpu.VMEM((FIELDS, *pad), F32),
            pltpu.VMEM((5, nt, h, LT), F32),
            pltpu.VMEM((2, nt, h, LT), jnp.int32),
            pltpu.VMEM((h, km), BF16),
            pltpu.VMEM((w, km), BF16),
            pltpu.VMEM((nblk, 2, kb, w), BF16),
            pltpu.VMEM((2, 4, 8, w), F32),
            pltpu.VMEM((2, 3, 8, w), F32),
            pltpu.VMEM((2, 2, 8, w), jnp.int32),
            pltpu.VMEM((FIELDS, group, LT), F32),
            pltpu.VMEM((2, FIELDS, group, LT), F32),
            pltpu.VMEM((4, FIELDS, 8, LT), F32),
            pltpu.VMEM((1, *pad), F32),
            pltpu.VMEM((2, *pad), F32),
            pltpu.VMEM((2, *pad), F32),
            pltpu.VMEM((2, *pad), F32),
            pltpu.VMEM((2, *pad), F32),
            pltpu.VMEM((h, w), BF16),
            pltpu.VMEM((steps, nblk, kb, BLOCK), F32),
            pltpu.VMEM((steps, nblk, kb, BLOCK), F32),
            pltpu.VMEM((steps, nblk, kb, BLOCK), F32),
            pltpu.VMEM((steps, nblk - 1, kb, BLOCK), F32),
            pltpu.VMEM((ngx, kb, ab), F32),
            pltpu.VMEM((ngx, kb, ab), F32),
            dma((nt, 7)),
            dma((2,)),
            dma((2, 7)),
            dma((2, 7)),
            dma((2, 2)),
            dma((2, 2)),
            dma((2, 4)),
            dma((2, 4)),
            dma((steps,)),
            dma((steps,)),
            dma((steps, nblk - 1)),
            dma((steps, nblk - 1)),
            dma((ngx,)),
            dma((ngx,)),
        ],
        compiler_params=pltpu.CompilerParams(
            collective_id=0, has_side_effects=True, vmem_limit_bytes=VMEM_LIMIT
        ),
    )(*args)
    adjoint = pltpu.with_memory_space_constraint(adjoint, pltpu.VMEM)
    coefficients = pltpu.with_memory_space_constraint(coefficients, pltpu.VMEM)
    adjoint, coefficients = pl.pallas_call(
        write_results,
        out_shape=(
            jax.ShapeDtypeStruct((2, h, w), F32),
            jax.ShapeDtypeStruct((kb, ab), F32),
        ),
        in_specs=[vmem_spec, vmem_spec],
        out_specs=(hbm_spec, hbm_spec),
        scratch_shapes=[dma((4,)), dma],
    )(adjoint, coefficients)
    return adjoint, coefficients.T


def solution(mesh):
    tile = P("gx", "gy")
    pair = P(None, "gx", "gy")
    return jax.shard_map(
        functools.partial(shards, mesh.shape["gx"], mesh.shape["gy"]),
        mesh=mesh,
        in_specs=(pair, pair, tile, tile, tile, tile, tile, P("gx", None), P("gy", None)),
        out_specs=(pair, tile),
        check_vma=False,
    )
```

```python
import functools

import jax
import jax.numpy as jnp
from jax import lax
from jax.experimental import pallas as pl
from jax.experimental.pallas import tpu as pltpu
from jax.sharding import PartitionSpec as P

SWEEPS = 3
LT = 128
DEEP = 4
LANES = 2 * DEEP
GROUPS = LT // LANES
TOP = 16
ROWS = 16
BLOCK = 128
EARLY = 2
FIELDS = 7
VMEM_LIMIT = 56 * 1024 * 1024
MESH = pl.DeviceIdType.MESH
F32 = jnp.float32
BF16 = jnp.bfloat16
U, V, ROOT, DRAG, FRONTS, RHS = 0, 1, 2, 3, 4, 5


def kernel(
    ngx, ngy,
    vel_h, obs_h, thick_h, rate_h, fric_h, mask_h, codes_h, mx_h, my_h,
    adj, coef_ref,
    d, raw_f, raw_i, mx, my, myt,
    ns_vel, ns_f, ns_i, pk_out, pk_in, corner_in,
    s_pad, q1, q2, p_f, g_f, grad,
    y_send, y_in, y_acc, g_in, z_out, z_in,
    load_sem, modes_sem, ns_send, ns_recv, pk_send, pk_recv, corner_send, corner_recv,
    y_ssem, y_rsem, g_ssem, g_rsem, z_send, z_recv,
):
    nt, h, _ = raw_i.shape[1:]
    w = nt * LT
    ring = nt + 1
    group = h // GROUPS
    ix, iy = lax.axis_index("gx"), lax.axis_index("gy")
    edge_tiles, inner_tiles = (0, nt - 1), tuple(range(1, nt - 1))

    def cols(t):
        return pl.ds(t * LT, LT)

    has_n, has_s, has_w, has_e = ix > 0, ix < ngx - 1, iy > 0, iy < ngy - 1
    diagonals = (
        (jnp.logical_and(has_n, has_w), -1, -1),
        (jnp.logical_and(has_n, has_e), -1, 1),
        (jnp.logical_and(has_s, has_w), 1, -1),
        (jnp.logical_and(has_s, has_e), 1, 1),
    )

    barrier = pltpu.get_barrier_semaphore()
    for off in range(1, ngx):
        pl.semaphore_signal(barrier, inc=1, device_id=(lax.rem(ix + off, ngx), iy), device_id_type=MESH)
    for off in range(1, ngy):
        pl.semaphore_signal(barrier, inc=1, device_id=(ix, lax.rem(iy + off, ngy)), device_id_type=MESH)
    near = 0
    for there, dx, dy in diagonals:
        near = near + there.astype(jnp.int32)

        @pl.when(there)
        def _(dx=dx, dy=dy):
            pl.semaphore_signal(barrier, inc=1, device_id=(ix + dx, iy + dy), device_id_type=MESH)

    loads = {}
    for t in edge_tiles + inner_tiles:
        pairs = [
            (vel_h.at[:, :, cols(t)], d.at[pl.ds(U, 2), t, pl.ds(TOP, h)]),
            (obs_h.at[:, :, cols(t)], raw_f.at[pl.ds(3, 2), t]),
            (thick_h.at[:, cols(t)], raw_f.at[0, t]),
            (rate_h.at[:, cols(t)], raw_f.at[1, t]),
            (fric_h.at[:, cols(t)], raw_f.at[2, t]),
            (mask_h.at[:, cols(t)], raw_i.at[0, t]),
            (codes_h.at[:, cols(t)], raw_i.at[1, t]),
        ]
        loads[t] = [pltpu.make_async_copy(src, dst, load_sem.at[t, n]) for n, (src, dst) in enumerate(pairs)]
    rigid, extra = (2, 3, 5), (1, 4, 6)
    for t in edge_tiles:
        loads[t][0].start()
    for n in range(1, 7):
        for t in edge_tiles:
            loads[t][n].start()
    for n in (0, *rigid, *extra):
        for t in inner_tiles:
            loads[t][n].start()
    modes = [pltpu.make_async_copy(my_h, my, modes_sem.at[0]), pltpu.make_async_copy(mx_h, mx, modes_sem.at[1])]
    for load in modes:
        load.start()

    def row_copies(side):
        there, step = ((has_s, 1), (has_n, -1))[side]
        rows, to = pl.ds((h - DEEP, 0)[side], DEEP), pl.ds((8 - DEEP, 0)[side], DEEP)
        few, few_to = pl.ds((h - 2, 0)[side], 2), pl.ds((6, 0)[side], 2)
        pairs = [
            (vel_h.at[:, rows], ns_vel.at[side, pl.ds(0, 2), to]),
            (obs_h.at[:, few], ns_vel.at[side, pl.ds(2, 2), few_to]),
            (thick_h.at[rows], ns_f.at[side, 0, to]),
            (rate_h.at[rows], ns_f.at[side, 1, to]),
            (fric_h.at[few], ns_f.at[side, 2, few_to]),
            (mask_h.at[rows], ns_i.at[side, 0, to]),
            (codes_h.at[few], ns_i.at[side, 1, few_to]),
        ]
        return there, [
            pltpu.make_async_remote_copy(
                src, dst, ns_send.at[side, n], ns_recv.at[side, n], device_id=(ix + step, iy), device_id_type=MESH)
            for n, (src, dst) in enumerate(pairs)
        ]

    parts = (pl.ds(0, 2), pl.ds(2, FIELDS - 2))

    def pack_copies(part):
        west = pltpu.make_async_remote_copy(
            pk_out.at[parts[part]], pk_in.at[1, parts[part]], pk_send.at[part, 0], pk_recv.at[part, 1],
            device_id=(ix, iy - 1), device_id_type=MESH)
        east = pltpu.make_async_remote_copy(
            pk_out.at[parts[part]], pk_in.at[0, parts[part]], pk_send.at[part, 1], pk_recv.at[part, 0],
            device_id=(ix, iy + 1), device_id_type=MESH)
        return [(has_w, west), (has_e, east)]

    def corner_copies(part):
        out = []
        for n, (there, dx, dy) in enumerate(diagonals):
            rows = pl.ds(0 if dx < 0 else group - DEEP, DEEP)
            to = pl.ds(0 if dx < 0 else 8 - DEEP, DEEP)
            out.append((there, pltpu.make_async_remote_copy(
                pk_out.at[parts[part], rows], corner_in.at[3 - n, parts[part], to],
                corner_send.at[part, n], corner_recv.at[part, 3 - n],
                device_id=(ix + dx, iy + dy), device_id_type=MESH)))
        return out

    for missing, side in ((ix == 0, 0), (ix == ngx - 1, 1)):

        @pl.when(missing)
        def _(side=side):
            ns_vel[side] = jnp.zeros(ns_vel.shape[1:], F32)
            ns_f[side] = jnp.zeros(ns_f.shape[1:], F32)
            ns_i[side] = jnp.zeros(ns_i.shape[1:], jnp.int32)

    for missing, side in ((iy == 0, 0), (iy == ngy - 1, 1)):

        @pl.when(missing)
        def _(side=side):
            pk_in[side] = jnp.zeros(pk_in.shape[1:], F32)

    for n, (there, _, _) in enumerate(diagonals):

        @pl.when(jnp.logical_not(there))
        def _(n=n):
            corner_in[n] = jnp.zeros(corner_in.shape[1:], F32)

    def aligned(r, by):
        return r if isinstance(r, int) else pl.multiple_of(r, by)

    def loop(step, first, last, stride=ROWS, unroll=2):
        def one(i, carry):
            step(pl.multiple_of(first + i * stride, 8))
            return carry

        lax.fori_loop(0, (last - first) // stride, one, 0, unroll=unroll)

    def root_of(kind, thick, rate):
        half = 0.5 * thick * rate
        return jnp.where(kind >= 1, half * lax.rsqrt(half), 0.0)

    def derive(kind, code, fric, vel, obs):
        ice = kind >= 1
        drag = jnp.where(kind == 2, fric, 0.0)
        pairs = code - (lax.shift_right_logical(code, 1) & 5)
        bits = (pairs & 3) + lax.shift_right_logical(pairs, 2)
        fronts = (2 * bits).astype(F32)
        return drag, fronts, jnp.where(ice, vel[0] - obs[0], 0.0), jnp.where(ice, vel[1] - obs[1], 0.0)

    def raw_root(t, r, rows):
        here = pl.ds(r, rows)
        return root_of(raw_i[0, t, here], raw_f[0, t, here], raw_f[1, t, here])

    def edge_root(side, t):
        return root_of(ns_i[side, 0, :, cols(t)], ns_f[side, 0, :, cols(t)], ns_f[side, 1, :, cols(t)])

    def prepare(tiles, rooted):
        def step(r):
            here, there = pl.ds(r, ROWS), pl.ds(r + TOP, ROWS)
            for t in tiles:
                if rooted:
                    d[ROOT, t, there] = raw_root(t, r, ROWS)
                out = derive(
                    raw_i[0, t, here], raw_i[1, t, here], raw_f[2, t, here],
                    [d[U, t, there], d[V, t, there]], [raw_f[3, t, here], raw_f[4, t, here]])
                for f, value in enumerate(out):
                    d[DRAG + f, t, there] = value

        loop(step, 0, h, unroll=8)

    lane = lax.broadcasted_iota(jnp.int32, (group, LT), 1)
    lane8 = lax.broadcasted_iota(jnp.int32, (8, LT), 1)
    slot = lax.rem(lane + LANES // 2, LT) // LANES

    def pack(f):
        value = None
        for n in range(GROUPS):
            here = pl.ds(TOP + n * group, group)
            part = jnp.where(lane < LT // 2, d[f, 0, here], d[f, nt - 1, here])
            by = LANES * (n + 1) % LT
            part = pltpu.roll(part, by, 1) if by else part
            value = part if value is None else jnp.where(slot == (n + 1) % GROUPS, part, value)
        pk_out[f] = value

    def unpack(f):
        value = jnp.where(lane % LANES < DEEP, pk_in[1, f], pk_in[0, f])
        for n in range(GROUPS):
            by = (LT - LANES * (n + 1)) % LT
            d[f, nt, pl.ds(TOP + n * group, group)] = pltpu.roll(value, by, 1) if by else value
        d[f, nt, pl.ds(TOP - 8, 8)] = jnp.where(lane8 < LT // 2, corner_in[1, f], corner_in[0, f])
        low = jnp.where(lane8 % LANES < DEEP, corner_in[3, f], corner_in[2, f])
        d[f, nt, pl.ds(TOP + h, 8)] = pltpu.roll(low, LT - LANES, 1)


    def neighbours(ref, c, r, t, rows=ROWS):
        lanes = lax.broadcasted_iota(jnp.int32, (rows, LT), 1)

        def near(tile):
            return ref[c, tile % ring, pl.ds(r, rows)]

        up = ref[c, t, pl.ds(r - 1, rows)]
        down = ref[c, t, pl.ds(r + 1, rows)]
        left = pltpu.roll(jnp.where(lanes == LT - 1, near(t - 1), near(t)), 1, 1)
        right = pltpu.roll(jnp.where(lanes == 0, near(t + 1), near(t)), LT - 1, 1)
        return up, down, left, right

    def weighted(ref, c, r, t):
        up, down, left, right = neighbours(ref, c, r, t)
        ns, ew = up + down, left + right
        return 4.0 * ns + ew if c == 0 else ns + 4.0 * ew

    def viscosity(r, rows=ROWS, side=None, tiles=tuple(range(ring))):
        here = pl.ds(r, rows)
        for t in tiles:
            up, down, left, right = neighbours(d, U, r, t, rows)
            ux, uy = down - up, right - left
            up, down, left, right = neighbours(d, V, r, t, rows)
            vx, vy = down - up, right - left
            shear = uy + vx
            strain = 0.25 * (ux * ux + vy * vy + ux * vy + 0.25 * (shear * shear))
            factor = jnp.exp2(jnp.log2(strain + 0.01) * (-1.0 / 6.0))
            if t < nt:
                if side is not None:
                    root = edge_root(side, t)
                elif t in edge_tiles:
                    root = d[ROOT, t, here]
                else:
                    root = raw_root(t, aligned(r - TOP, 8), rows)
                factor = root * factor
            s_pad[0, t, here] = factor

    def first(r):
        here = pl.ds(r, ROWS)
        for t in range(ring):
            up, down, left, right = neighbours(s_pad, 0, r, t)
            ns, ew = up + down, left + right
            s = s_pad[0, t, here]
            e = d[FRONTS, t, here] * (s * s) + d[DRAG, t, here] + 1.0
            for c, total in ((0, 4.0 * ns + ew), (1, ns + 4.0 * ew)):
                inverse = 1.0 / (s * total + e)
                value = d[RHS + c, t, here] * inverse
                p_f[c, t, here] = value
                g_f[c, t, here] = s * inverse
                q1[c, t, here] = s * value

    def second(r):
        here = pl.ds(r, ROWS)
        for t in range(ring):
            s = s_pad[0, t, here]
            for c in range(2):
                q2[c, t, here] = q1[c, t, here] + s * g_f[c, t, here] * weighted(q1, c, r, t)

    def third(r):
        here, there = pl.ds(aligned(r - TOP, ROWS), ROWS), pl.ds(r, ROWS)
        for t in range(nt):
            flux = None
            for c in range(2):
                value = p_f[c, t, there] + g_f[c, t, there] * weighted(q2, c, r, t)
                adj[c, here, cols(t)] = value
                term = d[c, t, there] * value
                flux = term if flux is None else flux + term
            grad[here, cols(t)] = (-d[DRAG, t, there] * flux).astype(BF16)

    nblk, _, kb, _ = myt.shape
    steps = h // BLOCK
    ab = mx.shape[1] // ngx
    core = lax.rem(iy, 2)
    cell = iy // 2
    rows_dims = (((1,), (1,)), ((), ()))

    def project(side, k):
        rows = myt[:, side].reshape(nblk * kb, w)
        here = pl.ds(pl.multiple_of(k * BLOCK, BLOCK), BLOCK)
        out = lax.dot_general(rows, grad[here, :], rows_dims, preferred_element_type=F32)
        return out.reshape(nblk, kb, BLOCK)

    def sibling_copy(k):
        return pltpu.make_async_remote_copy(
            y_send.at[k], y_in.at[k], y_ssem.at[k], y_rsem.at[k],
            device_id=(ix, iy + 1 - 2 * core), device_id_type=MESH)

    def partner(off):
        other = cell
        for bit in range(nblk.bit_length() - 1):
            if off >> bit & 1:
                other = other + (1 - 2 * lax.rem(cell // (1 << bit), 2)) * (1 << bit)
        return other

    def plane_copy(k, off):
        other = partner(off)
        return pltpu.make_async_remote_copy(
            y_acc.at[k, other], g_in.at[k, off - 1], g_ssem.at[k, off - 1], g_rsem.at[k, off - 1],
            device_id=(ix, 2 * other + core), device_id_type=MESH)

    def forward(k):
        sibling_copy(k).wait_recv()
        for off in range(nblk - 1, 0, -1):
            y_acc[k, partner(off)] += y_in[k, partner(off)]
            plane_copy(k, off).start()

    def start_sides(part):
        for there, copy in pack_copies(part) + corner_copies(part):

            @pl.when(there)
            def _(copy=copy):
                copy.start()

    def take_sides(part):
        (_, west), (_, east) = pack_copies(part)
        waits = [(has_w, east), (has_e, west)]
        waits += [(there, copy) for (there, _, _), (_, copy) in zip(diagonals, reversed(corner_copies(part)))]
        for there, copy in waits:

            @pl.when(there)
            def _(copy=copy):
                copy.wait_recv()

    for t in edge_tiles:
        loads[t][0].wait()
    pack(U)
    pack(V)
    pl.semaphore_wait(barrier, ngx - 1 + ngy - 1 + near)
    start_sides(0)
    for side in range(2):
        there, copies = row_copies(side)

        @pl.when(there)
        def _(copies=copies):
            for copy in copies:
                copy.start()

    for t in edge_tiles:
        for load in loads[t][1:]:
            load.wait()
    prepare(edge_tiles, True)
    for f in range(2, FIELDS):
        pack(f)
    start_sides(1)

    for n in (0, *rigid):
        for t in inner_tiles:
            loads[t][n].wait()
    tall = (h // ROWS - 2) * ROWS
    outer = (nt - 1, nt, 0)

    def rough(tiles):
        loop(lambda r: viscosity(r, tiles=tiles), TOP + 8, TOP + 8 + tall, unroll=10)
        viscosity(TOP + 8 + tall, tiles=tiles)

    rough(inner_tiles)
    for n in extra:
        for t in inner_tiles:
            loads[t][n].wait()
    prepare(inner_tiles, False)
    for load in modes:
        load.wait()
    myt[...] = my[...].T.reshape(myt.shape)

    take_sides(0)
    unpack(U)
    unpack(V)
    rough(outer)

    for side, there in ((0, has_n), (1, has_s)):
        copies = row_copies(side)[1]

        @pl.when(there)
        def _(copies=copies):
            for copy in copies:
                copy.wait_recv()

        rows = pl.ds((TOP - 8, TOP + h)[side], 8)
        for t in range(nt):
            vel = [ns_vel[side, n, :, cols(t)] for n in range(2)]
            out = derive(
                ns_i[side, 0, :, cols(t)], ns_i[side, 1, :, cols(t)], ns_f[side, 2, :, cols(t)],
                vel, [ns_vel[side, 2 + n, :, cols(t)] for n in range(2)])
            for f, value in zip((U, V, DRAG, FRONTS, RHS, RHS + 1), (*vel, *out)):
                d[f, t, rows] = value

    for side, r in ((0, TOP), (1, TOP + h - 8)):
        viscosity(r, 8)
        viscosity((r - 8, r + 8)[side], 8, side)

    take_sides(1)
    for f in range(2, FIELDS):
        unpack(f)
    ringed = pl.ds(TOP - 8, h + 16)
    s_pad[0, nt, ringed] = s_pad[0, nt, ringed] * d[ROOT, nt, ringed]

    def wave(n, parts="tsf"):
        if "t" in parts:
            third(aligned(TOP + (n - 4) * ROWS, ROWS))
        if "s" in parts:
            second(aligned(TOP - 8 + (n - 2) * ROWS, 8))
        if "f" in parts:
            first(aligned(TOP - 8 + n * ROWS, 8))

    per = BLOCK // ROWS
    half = per // 2

    def send_half(k):
        y_send[k] = project(1 - core, k)

    def keep_half(k):
        y_acc[k] = project(core, k)

    for n in range(4):
        wave(n, "f" if n < 2 else "sf")

    for n in range(per):
        wave(4 + n)

    for k in range(1, steps - 1):
        send_half(k - 1)
        for n in range(EARLY):
            wave(4 + k * per + n)
        sibling_copy(k - 1).start()
        if k >= 2:
            forward(k - 2)
        keep_half(k - 1)
        for n in range(EARLY, per):
            wave(4 + k * per + n)

    last = steps - 1
    send_half(last - 1)
    for n in range(EARLY):
        wave(4 + last * per + n)
    sibling_copy(last - 1).start()
    forward(last - 2)
    keep_half(last - 1)
    for n in range(EARLY, per):
        wave(4 + last * per + n, {per - 3: "ts", per - 2: "ts", per - 1: "t"}.get(n, "tsf"))
    send_half(last)
    sibling_copy(last).start()
    forward(last - 1)
    keep_half(last)
    forward(last)

    total = None
    for k in range(steps):
        rows = y_acc[k, cell] + y_in[k, cell]
        for off in range(1, nblk):
            plane_copy(k, off).wait_recv()
            rows = rows + g_in[k, off - 1]
        high = rows.astype(BF16)
        low = (rows - high.astype(F32)).astype(BF16)
        both = jnp.concatenate([high, low], axis=0)
        out = jnp.dot(both, mx[k * BLOCK : (k + 1) * BLOCK, :], preferred_element_type=F32)
        total = out if total is None else total + out
    total = total[:kb] + total[kb:]

    for n in range(ngx):
        z_out[n] = total[:, n * ab : (n + 1) * ab]

    for off in range(ngx - 1, 0, -1):
        for n in (ix - off, ix + off):

            @pl.when(jnp.logical_and(n >= 0, n < ngx))
            def _(n=n):
                pltpu.make_async_remote_copy(
                    z_out.at[n], z_in.at[ix], z_send.at[n], z_recv.at[ix],
                    device_id=(n, iy), device_id_type=MESH).start()

    def z_copy(n):
        return pltpu.make_async_remote_copy(
            z_out.at[n], z_in.at[n], z_send.at[n], z_recv.at[n],
            device_id=(n, iy), device_id_type=MESH)

    for side in range(2):
        there, copies = row_copies(side)

        @pl.when(there)
        def _(copies=copies):
            for copy in copies:
                copy.wait_send()

    for there, copy in pack_copies(0) + corner_copies(0) + pack_copies(1) + corner_copies(1):

        @pl.when(there)
        def _(copy=copy):
            copy.wait_send()

    for k in range(steps):
        sibling_copy(k).wait_send()
        for off in range(1, nblk):
            plane_copy(k, off).wait_send()

    coef_ref[...] = z_out[ix]
    for n in range(ngx):

        @pl.when(ix != n)
        def _(n=n):
            z_copy(n).wait_recv()
            coef_ref[...] += z_in[n]

    for n in range(ngx):

        @pl.when(ix != n)
        def _(n=n):
            z_copy(n).wait_send()


def write_results(adj, coef, adj_h, coef_h, adj_sem, coef_sem):
    rows = adj.shape[1] // 2
    copies = [pltpu.make_async_copy(coef, coef_h, coef_sem)]
    for n in range(4):
        part = (n % 2, pl.ds(n // 2 * rows, rows))
        copies.append(pltpu.make_async_copy(adj.at[part], adj_h.at[part], adj_sem.at[n]))
    for copy in copies:
        copy.start()
    for copy in copies:
        copy.wait()


def shards(ngx, ngy, velocity, observed, thickness, rate_factor, friction, cell_mask, front_codes, modes_x, modes_y):
    h, w = thickness.shape
    km = modes_x.shape[1]
    nt, nblk, kb, ab = w // LT, ngy // 2, km // ngy, km // ngx
    steps = h // BLOCK
    group = h // GROUPS
    hbm_spec = pl.BlockSpec(memory_space=pltpu.HBM)
    vmem_spec = pl.BlockSpec(memory_space=pltpu.VMEM)
    pad = (nt + 1, h + 2 * TOP, LT)
    dma = pltpu.SemaphoreType.DMA
    args = (velocity, observed, thickness, rate_factor, friction, cell_mask, front_codes, modes_x, modes_y)
    args = [pltpu.with_memory_space_constraint(x, pltpu.HBM) for x in args]
    adjoint, coefficients = pl.pallas_call(
        functools.partial(kernel, ngx, ngy),
        out_shape=(pltpu.VMEM((2, h, w), F32), pltpu.VMEM((kb, ab), F32)),
        in_specs=[hbm_spec] * 9,
        out_specs=(vmem_spec, vmem_spec),
        scratch_shapes=[
            pltpu.VMEM((FIELDS, *pad), F32),
            pltpu.VMEM((5, nt, h, LT), F32),
            pltpu.VMEM((2, nt, h, LT), jnp.int32),
            pltpu.VMEM((h, km), BF16),
            pltpu.VMEM((w, km), BF16),
            pltpu.VMEM((nblk, 2, kb, w), BF16),
            pltpu.VMEM((2, 4, 8, w), F32),
            pltpu.VMEM((2, 3, 8, w), F32),
            pltpu.VMEM((2, 2, 8, w), jnp.int32),
            pltpu.VMEM((FIELDS, group, LT), F32),
            pltpu.VMEM((2, FIELDS, group, LT), F32),
            pltpu.VMEM((4, FIELDS, 8, LT), F32),
            pltpu.VMEM((1, *pad), F32),
            pltpu.VMEM((2, *pad), F32),
            pltpu.VMEM((2, *pad), F32),
            pltpu.VMEM((2, *pad), F32),
            pltpu.VMEM((2, *pad), F32),
            pltpu.VMEM((h, w), BF16),
            pltpu.VMEM((steps, nblk, kb, BLOCK), F32),
            pltpu.VMEM((steps, nblk, kb, BLOCK), F32),
            pltpu.VMEM((steps, nblk, kb, BLOCK), F32),
            pltpu.VMEM((steps, nblk - 1, kb, BLOCK), F32),
            pltpu.VMEM((ngx, kb, ab), F32),
            pltpu.VMEM((ngx, kb, ab), F32),
            dma((nt, 7)),
            dma((2,)),
            dma((2, 7)),
            dma((2, 7)),
            dma((2, 2)),
            dma((2, 2)),
            dma((2, 4)),
            dma((2, 4)),
            dma((steps,)),
            dma((steps,)),
            dma((steps, nblk - 1)),
            dma((steps, nblk - 1)),
            dma((ngx,)),
            dma((ngx,)),
        ],
        compiler_params=pltpu.CompilerParams(
            collective_id=0, has_side_effects=True, vmem_limit_bytes=VMEM_LIMIT
        ),
    )(*args)
    adjoint = pltpu.with_memory_space_constraint(adjoint, pltpu.VMEM)
    coefficients = pltpu.with_memory_space_constraint(coefficients, pltpu.VMEM)
    adjoint, coefficients = pl.pallas_call(
        write_results,
        out_shape=(
            jax.ShapeDtypeStruct((2, h, w), F32),
            jax.ShapeDtypeStruct((kb, ab), F32),
        ),
        in_specs=[vmem_spec, vmem_spec],
        out_specs=(hbm_spec, hbm_spec),
        scratch_shapes=[dma((4,)), dma],
    )(adjoint, coefficients)
    return adjoint, coefficients.T


def solution(mesh):
    tile = P("gx", "gy")
    pair = P(None, "gx", "gy")
    return jax.shard_map(
        functools.partial(shards, mesh.shape["gx"], mesh.shape["gy"]),
        mesh=mesh,
        in_specs=(pair, pair, tile, tile, tile, tile, tile, P("gx", None), P("gy", None)),
        out_specs=(pair, tile),
        check_vma=False,
    )
```
